128 devices in a mesh: dp: 8 (over y_hi, x), mp: 16 (over y_lo, z, core).
Axes of the slice: x: 4, y: 4 (y_hi: 2, y_lo: 2; y = y_hi * 2 + y_lo), z: 4, core: 2. Of those that a mesh axis runs over, the one named last changes fastest.
Arguments:
- tokens: bfloat16 [4096, 4096], P('dp', 'mp'), may hold values from -6 to 6
- cotangent: bfloat16 [4096, 4096], P('dp', 'mp'), may hold values from -6 to 6
- w_in: bfloat16 [2, 4096, 10240], P(None, None, 'mp'), may hold values from -0.09375 to 0.09375
- w_out: bfloat16 [10240, 4096], P('mp'), may hold values from -0.0625 to 0.0625
- row_in: float32 [2, 4096], P(None, 'dp'), may hold values from 0.01 to 2
- col_in: float32 [2, 10240], P(None, 'mp'), may hold values from 0.01 to 2
- row_out: float32 [10240], P('mp'), may hold values from 0.01 to 2
- col_out: float32 [4096], P('dp'), may hold values from 0.01 to 2
Outputs:
- input_grad: bfloat16 [4096, 4096], P('dp', 'mp')
- update_in: bfloat16 [2, 4096, 10240], P(None, 'dp', 'mp')
- update_out: bfloat16 [10240, 4096], P('mp', 'dp')
- row_in_new: float32 [2, 4096], P(None, 'dp')
- col_in_new: float32 [2, 10240], P(None, 'mp')
- row_out_new: float32 [10240], P('mp')
- col_out_new: float32 [4096], P('dp')
The draws below stay inside these ranges and needn't reach their ends.
All inputs are finite; a program needn't handle non-finite values.
Results may differ from the reference program's by a relative error of at most 0.025.
Values may be sent and summed in bfloat16 or wider, within the bound.
A program may use at most 128 MiB of HBM per device.

```python
import math
import jax
import jax.numpy as jnp
from jax import lax

D = 4096
FF = 10240
TOK_DEV = 512
TOKENS = 4096
N_DP = 8
N_MP = 16


def shard_levels(stream_key, dims, split, least, largest):
    def one(position, parts):
        steps = jax.random.uniform(jax.random.fold_in(jax.random.fold_in(stream_key, 6), position), (parts,), jnp.float32, least / len(split), largest / len(split))
        return jnp.repeat(jnp.exp(steps), dims[position] // parts).reshape((-1,) + (1,) * (len(dims) - position - 1))

    loudness = one(*split[0])
    for cut in split[1:]:
        loudness = loudness * one(*cut)
    return loudness


def noise(stream_key, shape, deviation, bound, shards=(), held_as=jnp.bfloat16):
    drawn = jax.random.normal(stream_key, shape, jnp.float32) * deviation
    if len(shards) > 0:
        drawn = shard_levels(stream_key, shape, shards, -0.22, 0.18) * drawn
    return jnp.clip(drawn, min=-bound, max=bound).astype(held_as)


def setup_inputs(seed: int = 0) -> dict:
    key_of = jax.random.split(jax.random.key(seed), 9)
    return {
        "tokens": noise(key_of[0], (TOKENS, D), 1.0, 6.0, ((0, 8), (1, 16))),
        "cotangent": noise(key_of[1], (TOKENS, D), 1.0, 6.0, ((0, 8), (1, 16))),
        "w_in": noise(key_of[2], (2, D, FF), D ** -0.5, 0.09375, ((2, 16),)),
        "w_out": noise(key_of[3], (FF, D), FF ** -0.5, 0.0625, ((0, 16),)),
        "row_in": jnp.clip(jnp.exp(math.log(2.0) - 5.2983174 * jax.random.uniform(key_of[4], (2, D), jnp.float32) ** shard_levels(key_of[4], (2, D), ((1, 8),), -0.2, 0.2)), 0.01, 2.0),
        "col_in": jnp.clip(jnp.exp(math.log(2.0) - 5.2983174 * jax.random.uniform(key_of[5], (2, FF), jnp.float32) ** shard_levels(key_of[5], (2, FF), ((1, 16),), -0.2, 0.2)), 0.01, 2.0),
        "row_out": jnp.clip(jnp.exp(math.log(2.0) - 5.2983174 * jax.random.uniform(key_of[6], (FF,), jnp.float32) ** shard_levels(key_of[6], (FF,), ((0, 16),), -0.2, 0.2)), 0.01, 2.0),
        "col_out": jnp.clip(jnp.exp(math.log(2.0) - 5.2983174 * jax.random.uniform(key_of[7], (D,), jnp.float32) ** shard_levels(key_of[7], (D,), ((0, 8),), -0.2, 0.2)), 0.01, 2.0),
    }


def gelu_pair(values):
    root = math.sqrt(2.0 / math.pi)
    tanh_val = jnp.tanh(root * (values + 0.044715 * values * values * values))
    activated = 0.5 * values * (1.0 + tanh_val)
    slopes = 0.5 * (1.0 + tanh_val) + 0.5 * values * (1.0 - tanh_val * tanh_val) * root * (1.0 + 3.0 * 0.044715 * values * values)
    return (activated, slopes)

def rounded(values):
    return lax.optimization_barrier(values.astype(jnp.bfloat16)).astype(jnp.float32)

def reference(tokens, cotangent, w_in, w_out, row_in, col_in, row_out, col_out):
    gate_pre = jnp.dot(tokens, w_in[0], preferred_element_type=jnp.float32)
    up_pre = jnp.dot(tokens, w_in[1], preferred_element_type=jnp.float32)
    activated, slopes = gelu_pair(gate_pre)
    hidden = (activated * up_pre).astype(jnp.bfloat16)
    d_hidden = jnp.dot(cotangent, w_out.T, preferred_element_type=jnp.float32)
    d_gate = (d_hidden * up_pre * slopes).astype(jnp.bfloat16)
    d_up = (d_hidden * activated).astype(jnp.bfloat16)
    hid_block = FF // N_MP

    def add_hidden(total, block_index):
        offset = (block_index * hid_block).astype(jnp.int32)
        gate_cols = lax.dynamic_slice_in_dim(d_gate, offset, hid_block, 1)
        up_cols = lax.dynamic_slice_in_dim(d_up, offset, hid_block, 1)
        w_gate = lax.dynamic_slice_in_dim(w_in[0], offset, hid_block, 1)
        w_lin = lax.dynamic_slice_in_dim(w_in[1], offset, hid_block, 1)
        term = jnp.dot(gate_cols, w_gate.T, preferred_element_type=jnp.float32) + jnp.dot(up_cols, w_lin.T, preferred_element_type=jnp.float32)
        return (total + rounded(term), None)
    input_total, unused = lax.scan(add_hidden, jnp.zeros((TOKENS, D), jnp.float32), jnp.arange(N_MP, dtype=jnp.int32))
    input_grad = input_total.astype(jnp.bfloat16)
    factor = 1.0 / math.sqrt(TOKENS)

    def add_block(totals, block_index):
        offset = (block_index * TOK_DEV).astype(jnp.int32)
        tok_rows = lax.dynamic_slice_in_dim(tokens, offset, TOK_DEV, 0)
        cot_rows = lax.dynamic_slice_in_dim(cotangent, offset, TOK_DEV, 0)
        gate_rows = lax.dynamic_slice_in_dim(d_gate, offset, TOK_DEV, 0)
        up_rows = lax.dynamic_slice_in_dim(d_up, offset, TOK_DEV, 0)
        hid_rows = lax.dynamic_slice_in_dim(hidden, offset, TOK_DEV, 0)
        first = rounded(jnp.dot(tok_rows.T, gate_rows, preferred_element_type=jnp.float32) * factor)
        second = rounded(jnp.dot(tok_rows.T, up_rows, preferred_element_type=jnp.float32) * factor)
        third = rounded(jnp.dot(hid_rows.T, cot_rows, preferred_element_type=jnp.float32) * factor)
        return ((totals[0] + jnp.stack([first, second]), totals[1] + third), None)
    start_vals = (jnp.zeros((2, D, FF), jnp.float32), jnp.zeros((FF, D), jnp.float32))
    (grad_in, grad_out), unused2 = lax.scan(add_block, start_vals, jnp.arange(N_DP, dtype=jnp.int32))
    nu_in = jnp.minimum(row_in[:, :, None], col_in[:, None, :]) + grad_in * grad_in
    nu_out = jnp.minimum(row_out[:, None], col_out[None, :]) + grad_out * grad_out
    row_in_new = lax.optimization_barrier(jnp.max(nu_in, axis=2))
    col_in_new = lax.optimization_barrier(jnp.max(nu_in, axis=1))
    row_out_new = lax.optimization_barrier(jnp.max(nu_out, axis=1))
    col_out_new = lax.optimization_barrier(jnp.max(nu_out, axis=0))
    update_in = (grad_in / jnp.sqrt(nu_in)).astype(jnp.bfloat16)
    update_out = (grad_out / jnp.sqrt(nu_out)).astype(jnp.bfloat16)
    return (input_grad, update_in, update_out, row_in_new, col_in_new, row_out_new, col_out_new)
```

```python
import functools
import math

import jax
import jax.numpy as jnp
from jax import lax
from jax.experimental import pallas as pl
from jax.experimental.pallas import tpu as pltpu
from jax.sharding import PartitionSpec as P

BF = jnp.bfloat16
F32 = jnp.float32
MESH = pl.DeviceIdType.MESH
ROOT = math.sqrt(2.0 / math.pi)

HID, DUP, DGATE = 0, 1, 2


def nn(a, b):
    return jnp.dot(a, b, preferred_element_type=F32)


def nt(a, b):
    return lax.dot_general(a, b, (((1,), (1,)), ((), ())), preferred_element_type=F32)


def tn(a, b):
    return lax.dot_general(a, b, (((0,), (0,)), ((), ())), preferred_element_type=F32)


def kernel(
    factor,
    tok_in,
    cot_in,
    w_in,
    w_out,
    row_in,
    col_in,
    row_out,
    col_out,
    ig_o,
    upd_in_o,
    upd_out_o,
    row_in_o,
    col_in_o,
    row_out_o,
    col_out_o,
    full,
    wi,
    wo,
    pre,
    act,
    other,
    accs,
    gsend,
    grecv,
    igs,
    igr,
    igz,
    igy,
    rowv,
    rbuf,
    cbuf,
    lsem,
    ssem,
    rsem,
    xssem,
    xrsem,
):
    dp, mp = lax.axis_index("dp"), lax.axis_index("mp")
    yh, x = dp // 4, dp % 4
    yl, z, c = mp // 8, (mp // 2) % 4, mp % 2
    t_rows, h_cols = pre.shape[1], pre.shape[2]
    half = t_rows // 2

    def dev(dx=0, dyh=0, dyl=0, dz=0, dc=0):
        return (
            lax.rem(yh + dyh, 2) * 4 + lax.rem(x + dx, 4),
            lax.rem(yl + dyl, 2) * 8 + lax.rem(z + dz, 4) * 2 + lax.rem(c + dc, 2),
        )

    def chip(dy, dz):
        return lax.rem(yl + dy, 2) * 4 + lax.rem(z + dz, 4)

    peers = [
        dev(dz=1), dev(dz=3), dev(dz=2), dev(dyl=1), dev(dc=1), dev(dyl=1, dc=1),
        dev(dx=1), dev(dx=3), dev(dx=2), dev(dyh=1),
    ]
    barrier = pltpu.get_barrier_semaphore()
    for peer in peers:
        pl.semaphore_signal(barrier, inc=1, device_id=peer, device_id_type=MESH)

    loads = []

    def load(src, dst):
        copy = pltpu.make_async_copy(src, dst, lsem.at[len(loads)])
        copy.start()
        loads.append(copy)
        return copy

    own_tok = load(tok_in, full.at[0, mp])
    own_cot = load(cot_in, full.at[1, mp])
    load_w = [load(w_in.at[0], wi.at[0]), load(w_in.at[1], wi.at[1])]
    load_wo = load(w_out, wo)

    sent = []

    def send(src, dst, device):
        i = len(sent)
        copy = pltpu.make_async_remote_copy(
            src_ref=src, dst_ref=dst, send_sem=ssem.at[i], recv_sem=rsem.at[i],
            device_id=device, device_id_type=MESH,
        )
        copy.start()
        sent.append(copy)
        return copy

    xsent = [[], []]

    def xsend(t, dy, dz, src=None):
        origin_z = lax.rem(z + dz, 4)
        origin_y = lax.rem(yl + dy, 2)
        dx = lax.rem(origin_z + 4 - x, 4)
        there = jnp.maximum(dx - 1, 0)
        i = len(xsent[t])
        copy = pltpu.make_async_remote_copy(
            src_ref=full.at[t, chip(dy, dz) * 2 + c] if src is None else src,
            dst_ref=other.at[t, there, origin_y, c],
            send_sem=xssem.at[t, i], recv_sem=xrsem.at[t, there, origin_y],
            device_id=(yh * 4 + origin_z, mp), device_id_type=MESH,
        )
        xsent[t].append((dx != 0, copy))

        @pl.when(dx != 0)
        def _():
            copy.start()

    ag = [{}, {}]
    sib = [{}, {}]

    def share(t, dy, dz, src=None):
        slot = full.at[t, chip(dy, dz) * 2 + c]
        sib[t][(dy, dz)] = send(slot if src is None else src, slot, dev(dc=1))
        xsend(t, dy, dz, src)

    def ag_start(t):
        src = tok_in if t == 0 else cot_in
        slot = full.at[t, mp]
        ag[t]["z-"] = send(src, slot, dev(dz=1))
        ag[t]["z+"] = send(src, slot, dev(dz=3))
        ag[t]["y"] = send(src, slot, dev(dyl=1))
        share(t, 0, 0, src)

    def ag_1(t):
        ag[t]["z-"].wait_recv()
        slot = full.at[t, chip(0, 3) * 2 + c]
        ag[t]["zz-"] = send(slot.at[pl.ds(0, half)], slot.at[pl.ds(0, half)], dev(dz=1))
        share(t, 0, 3)
        ag[t]["z+"].wait_recv()
        slot = full.at[t, chip(0, 1) * 2 + c]
        ag[t]["zz+"] = send(slot.at[pl.ds(half, half)], slot.at[pl.ds(half, half)], dev(dz=3))
        share(t, 0, 1)
        ag[t]["y"].wait_recv()
        slot = full.at[t, chip(1, 0) * 2 + c]
        ag[t]["yz-"] = send(slot, slot, dev(dz=1))
        ag[t]["yz+"] = send(slot, slot, dev(dz=3))
        share(t, 1, 0)

    def ag_2a(t):
        slot = full.at[t, chip(0, 2) * 2 + c]
        ag[t]["zz-"].wait_recv()
        ag[t]["yzz-"] = send(slot.at[pl.ds(0, half)], slot.at[pl.ds(0, half)], dev(dyl=1))
        ag[t]["zz+"].wait_recv()
        ag[t]["yzz+"] = send(slot.at[pl.ds(half, half)], slot.at[pl.ds(half, half)], dev(dyl=1))
        share(t, 0, 2)

    def ag_2b(t):
        ag[t]["yz-"].wait_recv()
        share(t, 1, 3)
        ag[t]["yz+"].wait_recv()
        share(t, 1, 1)

    def ag_3(t):
        ag[t]["yzz-"].wait_recv()
        ag[t]["yzz+"].wait_recv()
        share(t, 1, 2)

    def forward(dy, dz, first=False):
        sib[0][(dy, dz)].wait_recv()
        m = chip(dy, dz)

        @pl.loop(0, 4)
        def _(i):
            k, rows = i // 2, pl.ds(pl.multiple_of((i % 2) * half, half), half)
            part = nn(full[0, m * 2, rows], wi[k, pl.ds(pl.multiple_of(m * 512, 512), 256)]) + nn(
                full[0, m * 2 + 1, rows], wi[k, pl.ds(pl.multiple_of(m * 512 + 256, 256), 256)]
            )
            if first:
                pre[k, rows] = part
            else:
                pre[k, rows] += part

    def backward(dy, dz, first=False):
        sib[1][(dy, dz)].wait_recv()
        m = chip(dy, dz)

        @pl.loop(0, 2)
        def _(i):
            rows = pl.ds(pl.multiple_of(i * half, half), half)
            part = nt(full[1, m * 2, rows], wo[:, pl.ds(pl.multiple_of(m * 512, 512), 256)]) + nt(
                full[1, m * 2 + 1, rows], wo[:, pl.ds(pl.multiple_of(m * 512 + 256, 256), 256)]
            )
            if first:
                pre[2, rows] = part
            else:
                pre[2, rows] += part

    step = 32

    def make_hidden():
        @pl.loop(0, t_rows // step)
        def _(i):
            rows = pl.ds(pl.multiple_of(i * step, step), step)
            v = pre[0, rows]
            up = pre[1, rows]
            t = jnp.tanh(ROOT * (v + 0.044715 * v * v * v))
            activated = 0.5 * v * (1.0 + t)
            slopes = 0.5 * (1.0 + t) + 0.5 * v * (1.0 - t * t) * ROOT * (
                1.0 + 3.0 * 0.044715 * v * v
            )
            act[HID, 0, rows] = (activated * up).astype(BF)
            pre[0, rows] = activated
            pre[1, rows] = up * slopes

    def make_d():
        @pl.loop(0, t_rows // step)
        def _(i):
            rows = pl.ds(pl.multiple_of(i * step, step), step)
            d = pre[2, rows]
            act[DUP, 0, rows] = (d * pre[0, rows]).astype(BF)
            act[DGATE, 0, rows] = (d * pre[1, rows]).astype(BF)

    xg = [{}, {}, {}]
    lo, hi = pl.ds(0, half), pl.ds(half, half)

    def xg_start(q):
        own = act.at[q, 0]
        xg[q]["a-"] = send(own.at[lo], act.at[q, 1].at[lo], dev(dx=1))
        xg[q]["b+"] = send(own.at[hi], act.at[q, 3].at[hi], dev(dx=3))
        xg[q]["b-"] = send(own.at[hi], act.at[q, 1].at[hi], dev(dx=1))
        xg[q]["a+"] = send(own.at[lo], act.at[q, 3].at[lo], dev(dx=3))

    def xg_relay(q):
        xg[q]["a-"].wait_recv()
        xg[q]["aa"] = send(act.at[q, 1].at[lo], act.at[q, 2].at[lo], dev(dx=1))
        xg[q]["b+"].wait_recv()
        xg[q]["bb"] = send(act.at[q, 3].at[hi], act.at[q, 2].at[hi], dev(dx=3))

    def xg_rest(q):
        xg[q]["b-"].wait_recv()
        xg[q]["a+"].wait_recv()

    def xg_last(q):
        xg[q]["aa"].wait_recv()
        xg[q]["bb"].wait_recv()

    osib = [{}, {}]

    def other_share(t):
        for r in range(3):
            for h in range(2):
                slot = other.at[t, r, h, c]
                pltpu.make_async_remote_copy(
                    src_ref=slot, dst_ref=slot, send_sem=xssem.at[t, 0], recv_sem=xrsem.at[t, r, h],
                    device_id=dev(dc=1), device_id_type=MESH,
                ).wait_recv()
                osib[t][(r, h)] = send(slot, slot, dev(dc=1))

    def other_wait(t):
        for copy in osib[t].values():
            copy.wait_recv()

    gs = [None] * 3

    def wgrad(q, r, first=False, last=False):
        t = 1 if q == HID else 0

        @pl.loop(0, 4)
        def _(i):
            part_kept, b = i // 2, i % 2
            h = jnp.where(part_kept == 1, yh, 1 - yh)
            rows = pl.ds(pl.multiple_of(b * 256, 256), 256)
            if r == 0:
                left = full[t, 2 * x + 8 * h + b]
            else:
                left = other[t, r - 1, h, b]
            part = tn(left, act[q, r]) * factor

            @pl.when(part_kept == 1)
            def _():
                pre[q, rows] = part if first else pre[q, rows] + part

            @pl.when(part_kept == 0)
            def _():
                total = part if first else accs[rows] + part
                if last:
                    gsend[q, rows] = total.astype(BF)
                else:
                    accs[rows] = total

        if last:
            gs[q] = send(gsend.at[q], grecv.at[q], dev(dyh=1))

    def shard_rows(shard):
        return pl.ds(pl.multiple_of(shard * 256, 256), 256)

    igc = [None] * 8

    def ig_other(n, m):
        shard = 2 * m + 1 - c
        igs[m] = (
            nt(act[DGATE, 0], wi[0, shard_rows(shard)]) + nt(act[DUP, 0], wi[1, shard_rows(shard)])
        ).astype(BF)
        igc[n] = send(igs.at[m], igr.at[m], dev(dc=1))

    igzc = {}

    def ig_own(n, m):
        igc[n].wait_recv()
        shard = 2 * m + c
        total = nt(act[DGATE, 0], wi[0, shard_rows(shard)]) + nt(act[DUP, 0], wi[1, shard_rows(shard)])
        igr[m] = (total + igr[m].astype(F32)).astype(BF)

    def ig_final_1():
        for copy in igzc.values():
            copy.wait_recv()
        for y in (1, 0):
            m = chip(y, 0)
            total = igr[m].astype(F32)
            for r in range(3):
                total = total + igz[r, y].astype(F32)
            if y == 1:
                igy[0] = total.astype(BF)
                igzc["y"] = send(igy.at[0], igy.at[1], dev(dyl=1))
            else:
                pre[0, :, pl.ds(0, 256)] = total

    def ig_final_2():
        igzc["y"].wait_recv()
        ig_o[...] = (pre[0, :, pl.ds(0, 256)] + igy[1].astype(F32)).astype(BF)

    fin = 64

    def final(q):
        gs[q].wait_recv()
        if q == HID:
            col = row_out[...]
        else:
            col = col_in[pl.ds(2 - q, 1)]

        def body(i, colmax):
            rows = pl.ds(pl.multiple_of(i * fin, fin), fin)
            g = pre[q, rows] + grecv[q, rows].astype(F32)
            nu = jnp.minimum(rowv[q, rows][:, :1], col) + g * g
            upd = g * lax.rsqrt(nu)
            if q == HID:
                pre[q, rows] = upd
            else:
                upd_in_o[2 - q, rows] = upd.astype(BF)
            rowv[q, rows] = jnp.broadcast_to(jnp.max(nu, axis=1, keepdims=True), (fin, 128))
            return jnp.maximum(colmax, jnp.max(nu, axis=0, keepdims=True))

        colmax = lax.fori_loop(0, 512 // fin, body, jnp.zeros((1, h_cols), F32))
        cbuf[0, pl.ds(q, 1)] = colmax
        rbuf[0, pl.ds(q, 1), pl.ds(0, 512)] = rowv[q].T[:1]
        if q == HID:
            @pl.loop(0, h_cols // 128)
            def _(j):
                cols = pl.ds(pl.multiple_of(j * 128, 128), 128)
                upd_out_o[cols] = pre[q, :, cols].T.astype(BF)

    cbuf[0] = jnp.zeros_like(cbuf[0])
    rbuf[0] = jnp.zeros_like(rbuf[0])
    pl.semaphore_wait(barrier, len(peers))
    ag_start(0)
    for q in range(3):
        row = col_out[...] if q == HID else row_in[pl.ds(2 - q, 1)]
        rowv[q] = jnp.broadcast_to(row, (128, 512)).T
    own_tok.wait()
    own_cot.wait()
    ag_1(0)
    ag_start(1)
    for copy in load_w:
        copy.wait()
    forward(0, 0, first=True)
    ag_2a(0)
    forward(0, 3)
    forward(0, 1)
    ag_2b(0)
    forward(1, 0)
    forward(0, 2)
    ag_3(0)
    forward(1, 3)
    forward(1, 1)
    forward(1, 2)
    make_hidden()
    xg_start(HID)
    ag_1(1)
    load_wo.wait()
    backward(0, 0, first=True)
    ag_2a(1)
    backward(0, 3)
    backward(0, 1)
    ag_2b(1)
    backward(1, 0)
    backward(0, 2)
    ag_3(1)
    backward(1, 3)
    backward(1, 1)
    backward(1, 2)
    make_d()
    xg_start(DUP)
    xg_start(DGATE)
    xg_relay(HID)
    order = [(dy, dz) for dz in (2, 1, 3, 0) for dy in (1, 0)]
    for n, (dy, dz) in enumerate(order):
        ig_other(n, chip(dy, dz))
    other_share(0)
    for n, (dy, dz) in enumerate(order):
        ig_own(n, chip(dy, dz))
        if dz != 0:
            igzc[(dy, dz)] = send(igr.at[chip(dy, dz)], igz.at[dz - 1, dy], dev(dz=dz))
    other_share(1)
    other_wait(1)
    wgrad(HID, 0, first=True)
    xg_rest(HID)
    wgrad(HID, 1)
    wgrad(HID, 3)
    xg_last(HID)
    wgrad(HID, 2, last=True)
    xg_relay(DUP)
    other_wait(0)
    wgrad(DUP, 0, first=True)
    xg_rest(DUP)
    wgrad(DUP, 1)
    wgrad(DUP, 3)
    xg_relay(DGATE)
    xg_last(DUP)
    wgrad(DUP, 2, last=True)
    final(HID)
    ig_final_1()
    ig_final_2()
    wgrad(DGATE, 0, first=True)
    xg_rest(DGATE)
    wgrad(DGATE, 1)
    wgrad(DGATE, 3)
    final(DUP)
    xg_last(DGATE)
    wgrad(DGATE, 2, last=True)
    final(DGATE)

    first = [
        send(rbuf.at[0], rbuf.at[1], dev(dc=1)),
        send(rbuf.at[0], rbuf.at[2], dev(dyl=1)),
        send(rbuf.at[0], rbuf.at[3], dev(dyl=1, dc=1)),
        send(cbuf.at[0], cbuf.at[1], dev(dyh=1)),
    ]
    for copy in first:
        copy.wait_recv()
    rbuf[4] = jnp.maximum(jnp.maximum(rbuf[0], rbuf[1]), jnp.maximum(rbuf[2], rbuf[3]))
    cbuf[2] = jnp.maximum(cbuf[0], cbuf[1])
    second = []
    for r in range(1, 4):
        second.append(send(rbuf.at[4], rbuf.at[4 + r], dev(dz=r)))
        second.append(send(cbuf.at[2], cbuf.at[2 + r], dev(dx=r)))
    for copy in second:
        copy.wait_recv()
    rmax = jnp.maximum(jnp.maximum(rbuf[4], rbuf[5]), jnp.maximum(rbuf[6], rbuf[7]))
    cmax = jnp.maximum(jnp.maximum(cbuf[2], cbuf[3]), jnp.maximum(cbuf[4], cbuf[5]))
    col_out_o[...] = rmax[HID : HID + 1, :512]
    row_out_o[...] = cmax[HID : HID + 1]
    for q in (DUP, DGATE):
        row_in_o[pl.ds(2 - q, 1)] = rmax[q : q + 1, :512]
        col_in_o[pl.ds(2 - q, 1)] = cmax[q : q + 1]

    for copy in sent:
        copy.wait_send()
    for t in range(2):
        for taken, copy in xsent[t]:
            @pl.when(taken)
            def _(copy=copy):
                copy.wait_send()


def local(tokens, cotangent, w_in, w_out, row_in, col_in, row_out, col_out):
    t_rows, d_cols = tokens.shape
    h_cols = w_out.shape[0]
    factor = 1.0 / math.sqrt(t_rows * lax.axis_size("dp"))
    vmem = pl.BlockSpec(memory_space=pltpu.VMEM)
    hbm = pl.BlockSpec(memory_space=pl.ANY)
    shapes = (
        jax.ShapeDtypeStruct((t_rows, 256), BF),
        jax.ShapeDtypeStruct((2, 512, h_cols), BF),
        jax.ShapeDtypeStruct((h_cols, 512), BF),
        jax.ShapeDtypeStruct((2, 512), F32),
        jax.ShapeDtypeStruct((2, h_cols), F32),
        jax.ShapeDtypeStruct((1, h_cols), F32),
        jax.ShapeDtypeStruct((1, 512), F32),
    )
    out = pl.pallas_call(
        functools.partial(kernel, factor),
        out_shape=shapes,
        in_specs=[hbm] * 4 + [vmem] * 4,
        out_specs=[vmem] * 7,
        scratch_shapes=[
            pltpu.VMEM((2, 16, t_rows, 256), BF),
            pltpu.VMEM(w_in.shape, BF),
            pltpu.VMEM(w_out.shape, BF),
            pltpu.VMEM((3, t_rows, h_cols), F32),
            pltpu.VMEM((3, 4, t_rows, h_cols), BF),
            pltpu.VMEM((2, 3, 2, 2, t_rows, 256), BF),
            pltpu.VMEM((512, h_cols), F32),
            pltpu.VMEM((3, 512, h_cols), BF),
            pltpu.VMEM((3, 512, h_cols), BF),
            pltpu.VMEM((8, t_rows, 256), BF),
            pltpu.VMEM((8, t_rows, 256), BF),
            pltpu.VMEM((3, 2, t_rows, 256), BF),
            pltpu.VMEM((2, t_rows, 256), BF),
            pltpu.VMEM((3, 512, 128), F32),
            pltpu.VMEM((8, 8, h_cols), F32),
            pltpu.VMEM((6, 8, h_cols), F32),
            pltpu.SemaphoreType.DMA((8,)),
            pltpu.SemaphoreType.DMA((100,)),
            pltpu.SemaphoreType.DMA((100,)),
            pltpu.SemaphoreType.DMA((2, 8)),
            pltpu.SemaphoreType.DMA((2, 3, 2)),
        ],
        compiler_params=pltpu.CompilerParams(
            collective_id=0, has_side_effects=True, vmem_limit_bytes=62 * 2**20
        ),
        cost_estimate=pl.CostEstimate(
            flops=21_500_000_000, bytes_accessed=22_000_000, transcendentals=330_000
        ),
    )(
        tokens, cotangent, w_in, w_out, row_in, col_in,
        row_out.reshape(1, h_cols), col_out.reshape(1, 512),
    )
    ig, upd_in, upd_out, row_in_new, col_in_new, row_out_new, col_out_new = out
    return (
        ig, upd_in, upd_out, row_in_new, col_in_new,
        row_out_new.reshape(h_cols), col_out_new.reshape(512),
    )


def solution(mesh):
    return jax.shard_map(
        local,
        mesh=mesh,
        in_specs=(
            P("dp", "mp"),
            P("dp", "mp"),
            P(None, None, "mp"),
            P("mp", None),
            P(None, "dp"),
            P(None, "mp"),
            P("mp"),
            P("dp"),
        ),
        out_specs=(
            P("dp", "mp"),
            P(None, "dp", "mp"),
            P("mp", "dp"),
            P(None, "dp"),
            P(None, "mp"),
            P("mp"),
            P("dp"),
        ),
        check_vma=False,
    )
```

```python
import functools
import math

import jax
import jax.numpy as jnp
from jax import lax
from jax.experimental import pallas as pl
from jax.experimental.pallas import tpu as pltpu
from jax.sharding import PartitionSpec as P

BF = jnp.bfloat16
F32 = jnp.float32
MESH = pl.DeviceIdType.MESH
ROOT = math.sqrt(2.0 / math.pi)

HID, DUP, DGATE = 0, 1, 2
PIECES = ((HID, 0, 640), (DUP, 0, 640), (DGATE, 0, 384), (DGATE, 384, 256))


def nn(a, b):
    return jnp.dot(a, b, preferred_element_type=F32)


def nt(a, b):
    return lax.dot_general(a, b, (((1,), (1,)), ((), ())), preferred_element_type=F32)


def tn(a, b):
    return lax.dot_general(a, b, (((0,), (0,)), ((), ())), preferred_element_type=F32)


def kernel(
    factor,
    tok_in,
    cot_in,
    w_in,
    w_out,
    row_in,
    col_in,
    row_out,
    col_out,
    ig_o,
    upd_in_o,
    upd_out_o,
    rmax_o,
    cmax_o,
    full,
    wi,
    wo,
    pre,
    act,
    other,
    accs,
    gsend,
    grecv,
    igs,
    igr,
    igz,
    igy,
    rowv,
    rowm,
    rbuf,
    cbuf,
    lsem,
    ssem,
    rsem,
    xssem,
    xrsem,
):
    dp, mp = lax.axis_index("dp"), lax.axis_index("mp")
    yh, x = dp // 4, dp % 4
    yl, z, c = mp // 8, (mp // 2) % 4, mp % 2
    t_rows, h_cols = pre.shape[1], pre.shape[2]
    half = t_rows // 2

    def dev(dx=0, dyh=0, dyl=0, dz=0, dc=0):
        return (
            lax.rem(yh + dyh, 2) * 4 + lax.rem(x + dx, 4),
            lax.rem(yl + dyl, 2) * 8 + lax.rem(z + dz, 4) * 2 + lax.rem(c + dc, 2),
        )

    def chip(dy, dz):
        return lax.rem(yl + dy, 2) * 4 + lax.rem(z + dz, 4)

    peers = [
        dev(dz=1), dev(dz=3), dev(dz=2), dev(dyl=1), dev(dc=1), dev(dyl=1, dc=1),
        dev(dx=1), dev(dx=3), dev(dx=2), dev(dyh=1),
    ]
    barrier = pltpu.get_barrier_semaphore()
    for peer in peers:
        pl.semaphore_signal(barrier, inc=1, device_id=peer, device_id_type=MESH)

    loads = []

    def load(src, dst):
        copy = pltpu.make_async_copy(src, dst, lsem.at[len(loads)])
        copy.start()
        loads.append(copy)
        return copy

    own_tok = load(tok_in, full.at[0, yl, z * 2 + c])
    own_cot = load(cot_in, full.at[1, yl, z * 2 + c])
    load_w = [load(w_in.at[0], wi.at[0]), load(w_in.at[1], wi.at[1])]
    load_wo = load(w_out, wo)

    sent = []

    def send(src, dst, device):
        i = len(sent)
        copy = pltpu.make_async_remote_copy(
            src_ref=src, dst_ref=dst, send_sem=ssem.at[i], recv_sem=rsem.at[i],
            device_id=device, device_id_type=MESH,
        )
        copy.start()
        sent.append(copy)
        return copy

    xsent = [[], []]

    def xsend(t, dy, dz, src):
        origin_z = lax.rem(z + dz, 4)
        origin_y = lax.rem(yl + dy, 2)
        dx = lax.rem(origin_z + 4 - x, 4)
        there = dx // 2 * 2
        i = len(xsent[t])
        copy = pltpu.make_async_remote_copy(
            src_ref=src,
            dst_ref=other.at[t, there, origin_y, c],
            send_sem=xssem.at[t, i], recv_sem=xrsem.at[t, there // 2, origin_y],
            device_id=(yh * 4 + origin_z, mp), device_id_type=MESH,
        )
        xsent[t].append((dx % 2 == 1, copy))

        @pl.when(dx % 2 == 1)
        def _():
            copy.start()

    sib = [{}, {}]

    class Gather:
        def __init__(self, slot, share):
            self.slot, self.share, self.got = slot, share, {}

        def push(self, name, dy, dz, part, device, src=None):
            slot = self.slot(dy, dz, part)
            self.got[name] = send(slot if src is None else src, slot, device)

        def start(self, src=None):
            self.push("z-", 0, 0, None, dev(dz=1), src)
            self.push("z+", 0, 0, None, dev(dz=3), src)
            self.push("y", 0, 0, None, dev(dyl=1), src)
            self.share(0, 0, src)

        def one(self):
            self.got["z-"].wait_recv()
            self.push("zz-", 0, 3, 0, dev(dz=1))
            self.share(0, 3, None)
            self.got["z+"].wait_recv()
            self.push("zz+", 0, 1, 1, dev(dz=3))
            self.share(0, 1, None)
            self.got["y"].wait_recv()
            self.push("yz-", 1, 0, None, dev(dz=1))
            self.push("yz+", 1, 0, None, dev(dz=3))
            self.share(1, 0, None)

        def two(self):
            self.got["zz-"].wait_recv()
            self.push("yzz-", 0, 2, 0, dev(dyl=1))
            self.got["zz+"].wait_recv()
            self.push("yzz+", 0, 2, 1, dev(dyl=1))
            self.share(0, 2, None)

        def three(self):
            self.got["yz-"].wait_recv()
            self.share(1, 3, None)
            self.got["yz+"].wait_recv()
            self.share(1, 1, None)

        def four(self):
            self.got["yzz-"].wait_recv()
            self.got["yzz+"].wait_recv()
            self.share(1, 2, None)

    def full_gather(t):
        def slot(dy, dz, part):
            ref = full.at[t, lax.rem(yl + dy, 2), lax.rem(z + dz, 4) * 2 + c]
            return ref if part is None else ref.at[pl.ds(part * half, half)]

        def share(dy, dz, src):
            ref = slot(dy, dz, None)
            sib[t][(dy, dz)] = send(ref if src is None else src, ref, dev(dc=1))
            xsend(t, dy, dz, ref if src is None else src)

        return Gather(slot, share)

    e2_rows = t_rows // 8

    def e2_slot(dy, dz, part):
        m = chip(dy, dz)
        if part is None:
            rows = pl.ds(pl.multiple_of(m * e2_rows, e2_rows), e2_rows)
        else:
            rows = pl.ds(
                pl.multiple_of(m * e2_rows + part * (e2_rows // 2), e2_rows // 2), e2_rows // 2
            )
        return other.at[:, 1, :, c, rows]

    ga, gb, ge = full_gather(0), full_gather(1), Gather(e2_slot, lambda dy, dz, src: None)
    e2 = []

    def e2_send():
        rows = pl.ds(pl.multiple_of(chip(0, 0) * e2_rows, e2_rows), e2_rows)
        e2.append(
            send(
                full.at[:, :, lax.rem(x + 2, 4) * 2 + c, rows],
                other.at[:, 1, :, c, rows],
                dev(dx=2),
            )
        )

    def e2_start():
        e2[0].wait_recv()
        ge.start()

    def forward(dy, dz, first=False):
        sib[0][(dy, dz)].wait_recv()
        m = chip(dy, dz)
        my, mz = lax.rem(yl + dy, 2), lax.rem(z + dz, 4) * 2

        @pl.loop(0, 4)
        def _(i):
            k, rows = i // 2, pl.ds(pl.multiple_of((i % 2) * half, half), half)
            part = nn(full[0, my, mz, rows], wi[k, pl.ds(pl.multiple_of(m * 512, 512), 256)]) + nn(
                full[0, my, mz + 1, rows], wi[k, pl.ds(pl.multiple_of(m * 512 + 256, 256), 256)]
            )
            if first:
                pre[k, rows] = part
            else:
                pre[k, rows] += part

    def backward(dy, dz, first=False):
        sib[1][(dy, dz)].wait_recv()
        m = chip(dy, dz)
        my, mz = lax.rem(yl + dy, 2), lax.rem(z + dz, 4) * 2

        @pl.loop(0, 2)
        def _(i):
            rows = pl.ds(pl.multiple_of(i * half, half), half)
            part = nt(full[1, my, mz, rows], wo[:, pl.ds(pl.multiple_of(m * 512, 512), 256)]) + nt(
                full[1, my, mz + 1, rows], wo[:, pl.ds(pl.multiple_of(m * 512 + 256, 256), 256)]
            )
            if first:
                pre[2, rows] = part
            else:
                pre[2, rows] += part

    step = 32

    def make_hidden():
        @pl.loop(0, t_rows // step)
        def _(i):
            rows = pl.ds(pl.multiple_of(i * step, step), step)
            v = pre[0, rows]
            up = pre[1, rows]
            t = jnp.tanh(ROOT * (v + 0.044715 * v * v * v))
            activated = 0.5 * v * (1.0 + t)
            slopes = 0.5 * (1.0 + t) + 0.5 * v * (1.0 - t * t) * ROOT * (
                1.0 + 3.0 * 0.044715 * v * v
            )
            act[HID, 0, rows] = (activated * up).astype(BF)
            pre[0, rows] = activated
            pre[1, rows] = up * slopes

    def make_d():
        @pl.loop(0, t_rows // step)
        def _(i):
            rows = pl.ds(pl.multiple_of(i * step, step), step)
            d = pre[2, rows]
            act[DUP, 0, rows] = (d * pre[0, rows]).astype(BF)
            act[DGATE, 0, rows] = (d * pre[1, rows]).astype(BF)

    xg = [{} for _ in PIECES]
    lo, hi = pl.ds(0, half), pl.ds(half, half)

    def xg_send(p, name, source, there, rows, device):
        q, first_col, cols = PIECES[p]
        cut = pl.ds(first_col, cols)
        xg[p][name] = send(act.at[q, source, rows, cut], act.at[q, there, rows, cut], device)

    def xg_start(p):
        xg_send(p, "a-", 0, 1, lo, dev(dx=1))
        xg_send(p, "b+", 0, 3, hi, dev(dx=3))
        xg_send(p, "b-", 0, 1, hi, dev(dx=1))
        xg_send(p, "a+", 0, 3, lo, dev(dx=3))

    def xg_relay(p):
        xg[p]["a-"].wait_recv()
        xg_send(p, "aa", 1, 2, lo, dev(dx=1))
        xg[p]["b+"].wait_recv()
        xg_send(p, "bb", 3, 2, hi, dev(dx=3))

    def xg_rest(p):
        xg[p]["b-"].wait_recv()
        xg[p]["a+"].wait_recv()

    def xg_last(p):
        xg[p]["aa"].wait_recv()
        xg[p]["bb"].wait_recv()

    osib = [[], []]

    def other_share(t):
        for r in (0, 2):
            for h in range(2):
                slot = other.at[t, r, h, c]
                pltpu.make_async_remote_copy(
                    src_ref=slot, dst_ref=slot, send_sem=xssem.at[t, 0],
                    recv_sem=xrsem.at[t, r // 2, h], device_id=dev(dc=1), device_id_type=MESH,
                ).wait_recv()
            slot = other.at[t, r, :, c]
            osib[t].append(send(slot, slot, dev(dc=1)))

    def e2_share():
        slot = other.at[:, 1, :, c]
        e2.append(send(slot, slot, dev(dc=1)))

    def other_wait(t):
        for copy in osib[t]:
            copy.wait_recv()

    def e2_wait():
        e2[1].wait_recv()

    gs = [None] * len(PIECES)

    def wgrad(p, r, first=False, last=False):
        q, first_col, n = PIECES[p]
        cut = pl.ds(first_col, n)
        t = 1 if q == HID else 0

        @pl.loop(0, 4)
        def _(i):
            part_kept, b = i // 2, i % 2
            h = jnp.where(part_kept == 1, yh, 1 - yh)
            rows = pl.ds(pl.multiple_of(b * 256, 256), 256)
            if r == 0:
                left = full[t, h, 2 * x + b]
            else:
                left = other[t, r - 1, h, b]
            part = tn(left, act[q, r, :, cut]) * factor

            @pl.when(part_kept == 1)
            def _():
                pre[q, rows, cut] = part if first else pre[q, rows, cut] + part

            @pl.when(part_kept == 0)
            def _():
                total = part if first else accs[rows, cut] + part
                if last:
                    gsend[q, rows, cut] = total.astype(BF)
                else:
                    accs[rows, cut] = total

        if last:
            gs[p] = send(gsend.at[q, :, cut], grecv.at[q, :, cut], dev(dyh=1))

    def shard_rows(shard):
        return pl.ds(pl.multiple_of(shard * 256, 256), 256)

    igc = [None] * 8

    def ig_other(n, m):
        shard = 2 * m + 1 - c
        igs[m] = (
            nt(act[DGATE, 0], wi[0, shard_rows(shard)]) + nt(act[DUP, 0], wi[1, shard_rows(shard)])
        ).astype(BF)
        igc[n] = send(igs.at[m], igr.at[m], dev(dc=1))

    igzc = {}

    def ig_own(n, m):
        igc[n].wait_recv()
        shard = 2 * m + c
        total = nt(act[DGATE, 0], wi[0, shard_rows(shard)]) + nt(act[DUP, 0], wi[1, shard_rows(shard)])
        igr[m] = (total + igr[m].astype(F32)).astype(BF)

    def ig_final_1():
        for copy in igzc.values():
            copy.wait_recv()
        for y in (1, 0):
            m = chip(y, 0)
            total = igr[m].astype(F32)
            for r in range(3):
                total = total + igz[r, y].astype(F32)
            if y == 1:
                igy[0] = total.astype(BF)
                igzc["y"] = send(igy.at[0], igy.at[1], dev(dyl=1))
            else:
                pre[0, :, pl.ds(0, 256)] = total

    def ig_final_2():
        igzc["y"].wait_recv()
        ig_o[...] = (pre[0, :, pl.ds(0, 256)] + igy[1].astype(F32)).astype(BF)

    fin = 64

    def final(p):
        q, first_col, n = PIECES[p]
        cut = pl.ds(first_col, n)
        gs[p].wait_recv()
        col = row_out[...].reshape(1, h_cols) if q == HID else col_in[pl.ds(2 - q, 1), cut]

        def body(i, colmax):
            rows = pl.ds(pl.multiple_of(i * fin, fin), fin)
            g = pre[q, rows, cut] + grecv[q, rows, cut].astype(F32)
            nu = jnp.minimum(rowv[q, rows][:, :1], col) + g * g
            upd = g * lax.rsqrt(nu)
            if q == HID:
                pre[q, rows] = upd
            else:
                upd_in_o[2 - q, rows, cut] = upd.astype(BF)
            rowm[p, rows] = jnp.broadcast_to(jnp.max(nu, axis=1, keepdims=True), (fin, 128))
            return jnp.maximum(colmax, jnp.max(nu, axis=0, keepdims=True))

        colmax = lax.fori_loop(0, 512 // fin, body, jnp.zeros((1, n), F32))
        cbuf[0, pl.ds(q, 1), cut] = colmax
        rowmax = rowm[p].T[:1]
        if first_col != 0:
            rowmax = jnp.maximum(rowmax, rbuf[0, pl.ds(q, 1), pl.ds(0, 512)])
        rbuf[0, pl.ds(q, 1), pl.ds(0, 512)] = rowmax
        if q == HID:
            @pl.loop(0, h_cols // 128)
            def _(j):
                cols = pl.ds(pl.multiple_of(j * 128, 128), 128)
                upd_out_o[cols] = pre[q, :, cols].T.astype(BF)

    cbuf[0] = jnp.zeros_like(cbuf[0])
    rbuf[0] = jnp.zeros_like(rbuf[0])
    pl.semaphore_wait(barrier, len(peers))
    ga.start(tok_in)
    for q in range(3):
        row = col_out[...].reshape(1, 512) if q == HID else row_in[pl.ds(2 - q, 1)]
        rowv[q] = jnp.broadcast_to(row, (128, 512)).T
    own_tok.wait()
    own_cot.wait()
    ga.one()
    gb.start(cot_in)
    for copy in load_w:
        copy.wait()
    forward(0, 0, first=True)
    ga.two()
    forward(0, 3)
    forward(0, 1)
    ga.three()
    forward(1, 0)
    forward(0, 2)
    ga.four()
    forward(1, 3)
    forward(1, 1)
    forward(1, 2)
    make_hidden()
    xg_start(0)
    gb.one()
    load_wo.wait()
    backward(0, 0, first=True)
    gb.two()
    backward(0, 3)
    backward(0, 1)
    gb.three()
    backward(1, 0)
    backward(0, 2)
    gb.four()
    e2_send()
    backward(1, 3)
    backward(1, 1)
    backward(1, 2)
    make_d()
    xg_relay(0)
    xg_start(1)
    order = [(dy, dz) for dz in (2, 1, 3, 0) for dy in (1, 0)]
    for n, (dy, dz) in enumerate(order[:4]):
        ig_other(n, chip(dy, dz))
    e2_start()
    for n, (dy, dz) in enumerate(order[4:]):
        ig_other(4 + n, chip(dy, dz))
    other_share(1)
    ge.one()
    xg_relay(1)
    xg_start(2)
    for n, (dy, dz) in enumerate(order):
        ig_own(n, chip(dy, dz))
        if dz != 0:
            igzc[(dy, dz)] = send(igr.at[chip(dy, dz)], igz.at[dz - 1, dy], dev(dz=dz))
        if n == 3:
            ge.two()
    ge.three()
    ge.four()
    e2_share()
    other_share(0)
    other_wait(1)
    wgrad(0, 0, first=True)
    xg_rest(0)
    wgrad(0, 1)
    wgrad(0, 3)
    xg_last(0)
    e2_wait()
    wgrad(0, 2, last=True)
    other_wait(0)
    wgrad(1, 0, first=True)
    xg_rest(1)
    wgrad(1, 1)
    wgrad(1, 3)
    xg_relay(2)
    xg_start(3)
    xg_last(1)
    wgrad(1, 2, last=True)
    final(0)
    ig_final_1()
    wgrad(2, 0, first=True)
    xg_rest(2)
    wgrad(2, 1)
    wgrad(2, 3)
    xg_relay(3)
    xg_last(2)
    wgrad(2, 2, last=True)
    ig_final_2()
    final(1)
    wgrad(3, 0, first=True)
    xg_rest(3)
    wgrad(3, 1)
    wgrad(3, 3)
    xg_last(3)
    wgrad(3, 2, last=True)
    final(2)
    final(3)

    first = [
        send(rbuf.at[0], rbuf.at[1], dev(dc=1)),
        send(rbuf.at[0], rbuf.at[2], dev(dyl=1)),
        send(rbuf.at[0], rbuf.at[3], dev(dyl=1, dc=1)),
        send(cbuf.at[0], cbuf.at[1], dev(dyh=1)),
    ]
    for copy in first:
        copy.wait_recv()
    rbuf[4] = jnp.maximum(jnp.maximum(rbuf[0], rbuf[1]), jnp.maximum(rbuf[2], rbuf[3]))
    cbuf[2] = jnp.maximum(cbuf[0], cbuf[1])
    second = []
    for r in range(1, 4):
        second.append(send(rbuf.at[4], rbuf.at[4 + r], dev(dz=r)))
        second.append(send(cbuf.at[2], cbuf.at[2 + r], dev(dx=r)))
    for copy in second:
        copy.wait_recv()
    rmax_o[...] = jnp.maximum(jnp.maximum(rbuf[4], rbuf[5]), jnp.maximum(rbuf[6], rbuf[7]))
    cmax_o[...] = jnp.maximum(jnp.maximum(cbuf[2], cbuf[3]), jnp.maximum(cbuf[4], cbuf[5]))

    for copy in sent:
        copy.wait_send()
    for t in range(2):
        for taken, copy in xsent[t]:
            @pl.when(taken)
            def _(copy=copy):
                copy.wait_send()


def finish(
    ig, upd_in, upd_out, rmax, cmax,
    ig_o, upd_in_o, upd_out_o, row_in_o, col_in_o, row_out_o, col_out_o,
    ig_v, upd_in_v, upd_out_v, sem,
):
    steps = ((ig, ig_v, ig_o), (upd_in, upd_in_v, upd_in_o), (upd_out, upd_out_v, upd_out_o))
    ins = [pltpu.make_async_copy(s, v, sem.at[0, i]) for i, (s, v, o) in enumerate(steps)]
    copies = [pltpu.make_async_copy(v, o, sem.at[1, i]) for i, (s, v, o) in enumerate(steps)]
    for copy in ins:
        copy.start()
    n = row_in_o.shape[1]
    col_out_o[...] = rmax[HID, pl.ds(0, n)]
    row_out_o[...] = cmax[HID]
    for q in (DUP, DGATE):
        row_in_o[pl.ds(2 - q, 1)] = rmax[q : q + 1, :n]
        col_in_o[pl.ds(2 - q, 1)] = cmax[q : q + 1]
    for before, copy in zip(ins, copies):
        before.wait()
        copy.start()
    for copy in copies:
        copy.wait()


def local(tokens, cotangent, w_in, w_out, row_in, col_in, row_out, col_out):
    t_rows, d_cols = tokens.shape
    h_cols = w_out.shape[0]
    factor = 1.0 / math.sqrt(t_rows * lax.axis_size("dp"))
    vmem = pl.BlockSpec(memory_space=pltpu.VMEM)
    hbm = pl.BlockSpec(memory_space=pl.ANY)
    shapes = (
        jax.ShapeDtypeStruct((t_rows, 256), BF),
        jax.ShapeDtypeStruct((2, 512, h_cols), BF),
        jax.ShapeDtypeStruct((h_cols, 512), BF),
        jax.ShapeDtypeStruct((8, h_cols), F32),
        jax.ShapeDtypeStruct((8, h_cols), F32),
    )
    out = pl.pallas_call(
        functools.partial(kernel, factor),
        out_shape=shapes,
        in_specs=[hbm] * 4 + [vmem] * 4,
        out_specs=[vmem] * 5,
        scratch_shapes=[
            pltpu.VMEM((2, 2, 8, t_rows, 256), BF),
            pltpu.VMEM(w_in.shape, BF),
            pltpu.VMEM(w_out.shape, BF),
            pltpu.VMEM((3, t_rows, h_cols), F32),
            pltpu.VMEM((3, 4, t_rows, h_cols), BF),
            pltpu.VMEM((2, 3, 2, 2, t_rows, 256), BF),
            pltpu.VMEM((512, h_cols), F32),
            pltpu.VMEM((3, 512, h_cols), BF),
            pltpu.VMEM((3, 512, h_cols), BF),
            pltpu.VMEM((8, t_rows, 256), BF),
            pltpu.VMEM((8, t_rows, 256), BF),
            pltpu.VMEM((3, 2, t_rows, 256), BF),
            pltpu.VMEM((2, t_rows, 256), BF),
            pltpu.VMEM((3, 512, 128), F32),
            pltpu.VMEM((4, 512, 128), F32),
            pltpu.VMEM((8, 8, h_cols), F32),
            pltpu.VMEM((6, 8, h_cols), F32),
            pltpu.SemaphoreType.DMA((8,)),
            pltpu.SemaphoreType.DMA((140,)),
            pltpu.SemaphoreType.DMA((140,)),
            pltpu.SemaphoreType.DMA((2, 8)),
            pltpu.SemaphoreType.DMA((2, 2, 2)),
        ],
        compiler_params=pltpu.CompilerParams(
            collective_id=0, has_side_effects=True, vmem_limit_bytes=62 * 2**20
        ),
        cost_estimate=pl.CostEstimate(
            flops=21_500_000_000, bytes_accessed=22_000_000, transcendentals=330_000
        ),
    )(tokens, cotangent, w_in, w_out, row_in, col_in, row_out, col_out)
    return pl.pallas_call(
        finish,
        out_shape=shapes[:3]
        + (
            jax.ShapeDtypeStruct(row_in.shape, F32),
            jax.ShapeDtypeStruct(col_in.shape, F32),
            jax.ShapeDtypeStruct(row_out.shape, F32),
            jax.ShapeDtypeStruct(col_out.shape, F32),
        ),
        in_specs=[hbm] * 3 + [vmem] * 2,
        out_specs=[hbm] * 3 + [vmem] * 4,
        scratch_shapes=[pltpu.VMEM(s.shape, BF) for s in shapes[:3]]
        + [pltpu.SemaphoreType.DMA((2, 3))],
    )(*out)


def solution(mesh):
    return jax.shard_map(
        local,
        mesh=mesh,
        in_specs=(
            P("dp", "mp"),
            P("dp", "mp"),
            P(None, None, "mp"),
            P("mp", None),
            P(None, "dp"),
            P(None, "mp"),
            P("mp"),
            P("dp"),
        ),
        out_specs=(
            P("dp", "mp"),
            P(None, "dp", "mp"),
            P("mp", "dp"),
            P(None, "dp"),
            P(None, "mp"),
            P("mp"),
            P("dp"),
        ),
        check_vma=False,
    )
```

```python
import functools
import math

import jax
import jax.numpy as jnp
from jax import lax
from jax.experimental import pallas as pl
from jax.experimental.pallas import tpu as pltpu
from jax.sharding import PartitionSpec as P

BF = jnp.bfloat16
F32 = jnp.float32
MESH = pl.DeviceIdType.MESH
ROOT = math.sqrt(2.0 / math.pi)

HID, DUP, DGATE = 0, 1, 2
MESSAGES = 133
SENDING = 48
PIECES = ((HID, 0, 640), (DUP, 0, 640), (DGATE, 0, 384), (DGATE, 384, 256))


def nn(a, b):
    return jnp.dot(a, b, preferred_element_type=F32)


def nt(a, b):
    return lax.dot_general(a, b, (((1,), (1,)), ((), ())), preferred_element_type=F32)


def tn(a, b):
    return lax.dot_general(a, b, (((0,), (0,)), ((), ())), preferred_element_type=F32)


def kernel(
    factor,
    tok_in,
    cot_in,
    w_in,
    w_out,
    row_in,
    col_in,
    row_out,
    col_out,
    ig_h,
    upd_in_h,
    upd_out_h,
    rmax_o,
    cmax_o,
    full,
    wi,
    wo,
    pre,
    act,
    other,
    accs,
    gsend,
    grecv,
    igs,
    igr,
    igz,
    igy,
    rowv,
    rowm,
    rbuf,
    cbuf,
    ig_o,
    upd_in_o,
    upd_out_o,
    lsem,
    ssem,
    rsem,
    xssem,
    xrsem,
):
    dp, mp = lax.axis_index("dp"), lax.axis_index("mp")
    yh, x = dp // 4, dp % 4
    yl, z, c = mp // 8, (mp // 2) % 4, mp % 2
    t_rows, h_cols = pre.shape[1], pre.shape[2]
    half = t_rows // 2

    def dev(dx=0, dyh=0, dyl=0, dz=0, dc=0):
        return (
            lax.rem(yh + dyh, 2) * 4 + lax.rem(x + dx, 4),
            lax.rem(yl + dyl, 2) * 8 + lax.rem(z + dz, 4) * 2 + lax.rem(c + dc, 2),
        )

    def chip(dy, dz):
        return lax.rem(yl + dy, 2) * 4 + lax.rem(z + dz, 4)

    peers = [
        dev(dz=1), dev(dz=3), dev(dz=2), dev(dyl=1), dev(dc=1), dev(dyl=1, dc=1),
        dev(dx=1), dev(dx=3), dev(dx=2), dev(dyh=1),
    ]
    barrier = pltpu.get_barrier_semaphore()
    for peer in peers:
        pl.semaphore_signal(barrier, inc=1, device_id=peer, device_id_type=MESH)

    loads = []

    def load(src, dst):
        copy = pltpu.make_async_copy(src, dst, lsem.at[len(loads)])
        copy.start()
        loads.append(copy)
        return copy

    own_tok = load(tok_in, full.at[0, yl, z * 2 + c])
    own_cot = load(cot_in, full.at[1, yl, z * 2 + c])

    sent = []

    def send(src, dst, device):
        i = len(sent)
        if i >= SENDING:
            sent[i - SENDING].wait_send()
        copy = pltpu.make_async_remote_copy(
            src_ref=src, dst_ref=dst, send_sem=ssem.at[i % SENDING], recv_sem=rsem.at[i],
            device_id=device, device_id_type=MESH,
        )
        copy.start()
        sent.append(copy)
        return copy

    xsent = []

    def xsend(dy, dz, src):
        origin_z = lax.rem(z + dz, 4)
        origin_y = lax.rem(yl + dy, 2)
        dx = lax.rem(origin_z + 4 - x, 4)
        there = dx // 2 * 2
        i = len(xsent)
        copy = pltpu.make_async_remote_copy(
            src_ref=src,
            dst_ref=other.at[0, there, origin_y, c],
            send_sem=xssem.at[i], recv_sem=xrsem.at[there // 2, origin_y],
            device_id=(yh * 4 + origin_z, mp), device_id_type=MESH,
        )
        xsent.append((dx % 2 == 1, copy))

        @pl.when(dx % 2 == 1)
        def _():
            copy.start()

    sib = [{}, {}]

    class Gather:
        def __init__(self, slot, share):
            self.slot, self.share, self.got = slot, share, {}

        def push(self, name, dy, dz, part, device, src=None):
            slot = self.slot(dy, dz, part)
            self.got[name] = send(slot if src is None else self.part_of(src, part), slot, device)

        def part_of(self, src, part):
            n = src.shape[0] // 2
            return src.at[pl.ds(part * n, n)]

        def wait(self, name):
            self.got[name].wait_recv()

        def start(self, src=None):
            self.push("z-0", 0, 0, 0, dev(dz=1), src)
            self.push("z+1", 0, 0, 1, dev(dz=3), src)
            self.push("y0", 0, 0, 0, dev(dyl=1), src)
            self.push("z-1", 0, 0, 1, dev(dz=1), src)
            self.push("z+0", 0, 0, 0, dev(dz=3), src)
            self.push("y1", 0, 0, 1, dev(dyl=1), src)
            self.share(0, 0, src)

        def one(self):
            self.wait("z-0")
            self.push("zz0", 0, 3, 0, dev(dz=1))
            self.wait("z+1")
            self.push("zz1", 0, 1, 1, dev(dz=3))
            self.wait("y0")
            self.push("yz-0", 1, 0, 0, dev(dz=1))
            self.push("yz+0", 1, 0, 0, dev(dz=3))
            self.wait("z-1")
            self.share(0, 3, None)
            self.wait("z+0")
            self.share(0, 1, None)
            self.wait("y1")
            self.push("yz-1", 1, 0, 1, dev(dz=1))
            self.push("yz+1", 1, 0, 1, dev(dz=3))
            self.share(1, 0, None)

        def two(self):
            self.wait("zz0")
            self.push("yzz0", 0, 2, 0, dev(dyl=1))
            self.wait("zz1")
            self.push("yzz1", 0, 2, 1, dev(dyl=1))
            self.share(0, 2, None)

        def three(self):
            self.wait("yz-0")
            self.wait("yz-1")
            self.share(1, 3, None)
            self.wait("yz+0")
            self.wait("yz+1")
            self.share(1, 1, None)

        def four(self):
            self.wait("yzz0")
            self.wait("yzz1")
            self.share(1, 2, None)

    def full_gather(t):
        def slot(dy, dz, part):
            ref = full.at[t, lax.rem(yl + dy, 2), lax.rem(z + dz, 4) * 2 + c]
            return ref if part is None else ref.at[pl.ds(part * half, half)]

        def share(dy, dz, src):
            ref = slot(dy, dz, None)
            sib[t][(dy, dz)] = send(ref if src is None else src, ref, dev(dc=1))
            if t == 0:
                xsend(dy, dz, ref if src is None else src)

        return Gather(slot, share)

    e2_rows = t_rows // 8
    far = ((1, 1), (0, 3))

    def e2_gather(t):
        first, count = far[t]

        def slot(dy, dz, part):
            n = e2_rows // 2
            rows = pl.ds(pl.multiple_of(chip(dy, dz) * e2_rows + part * n, n), n)
            return other.at[t, pl.ds(first, count), :, c, rows]

        return Gather(slot, lambda dy, dz, src: None)

    ga, gb = full_gather(0), full_gather(1)
    ge = [e2_gather(0), e2_gather(1)]
    e2 = [[], []]
    eshare = [None, None]

    def e2_send(t):
        rows = pl.ds(pl.multiple_of(chip(0, 0) * e2_rows, e2_rows), e2_rows)
        first, count = far[t]
        for r in range(first, first + count):
            e2[t].append(
                send(
                    full.at[t, :, lax.rem(x + r + 1, 4) * 2 + c, rows],
                    other.at[t, r, :, c, rows],
                    dev(dx=r + 1),
                )
            )

    def e2_start(t):
        for copy in e2[t]:
            copy.wait_recv()
        ge[t].start()

    def e2_share(t):
        first, count = far[t]
        slot = other.at[t, pl.ds(first, count), :, c]
        eshare[t] = send(slot, slot, dev(dc=1))

    def forward(dy, dz, first=False):
        sib[0][(dy, dz)].wait_recv()
        m = chip(dy, dz)
        my, mz = lax.rem(yl + dy, 2), lax.rem(z + dz, 4) * 2

        @pl.loop(0, 4)
        def _(i):
            k, rows = i // 2, pl.ds(pl.multiple_of((i % 2) * half, half), half)
            part = nn(full[0, my, mz, rows], wi[k, pl.ds(pl.multiple_of(m * 512, 512), 256)]) + nn(
                full[0, my, mz + 1, rows], wi[k, pl.ds(pl.multiple_of(m * 512 + 256, 256), 256)]
            )
            if first:
                pre[k, rows] = part
            else:
                pre[k, rows] += part

    def backward(dy, dz, first=False):
        sib[1][(dy, dz)].wait_recv()
        m = chip(dy, dz)
        my, mz = lax.rem(yl + dy, 2), lax.rem(z + dz, 4) * 2

        @pl.loop(0, 2)
        def _(i):
            rows = pl.ds(pl.multiple_of(i * half, half), half)
            part = nt(full[1, my, mz, rows], wo[:, pl.ds(pl.multiple_of(m * 512, 512), 256)]) + nt(
                full[1, my, mz + 1, rows], wo[:, pl.ds(pl.multiple_of(m * 512 + 256, 256), 256)]
            )
            if first:
                pre[2, rows] = part
            else:
                pre[2, rows] += part

    step = 32

    def make_hidden():
        @pl.loop(0, t_rows // step)
        def _(i):
            rows = pl.ds(pl.multiple_of(i * step, step), step)
            v = pre[0, rows]
            up = pre[1, rows]
            t = jnp.tanh(ROOT * (v + 0.044715 * v * v * v))
            activated = 0.5 * v * (1.0 + t)
            slopes = 0.5 * (1.0 + t) + 0.5 * v * (1.0 - t * t) * ROOT * (
                1.0 + 3.0 * 0.044715 * v * v
            )
            act[HID, 0, rows] = (activated * up).astype(BF)
            pre[0, rows] = activated
            pre[1, rows] = up * slopes

    def make_d():
        @pl.loop(0, t_rows // step)
        def _(i):
            rows = pl.ds(pl.multiple_of(i * step, step), step)
            d = pre[2, rows]
            act[DUP, 0, rows] = (d * pre[0, rows]).astype(BF)
            act[DGATE, 0, rows] = (d * pre[1, rows]).astype(BF)

    xg = [{} for _ in PIECES]
    lo, hi = pl.ds(0, half), pl.ds(half, half)

    def xg_send(p, name, source, there, rows, device):
        q, first_col, cols = PIECES[p]
        cut = pl.ds(first_col, cols)
        xg[p][name] = send(act.at[q, source, rows, cut], act.at[q, there, rows, cut], device)

    def xg_start(p):
        xg_send(p, "a-", 0, 1, lo, dev(dx=1))
        xg_send(p, "b+", 0, 3, hi, dev(dx=3))
        xg_send(p, "b-", 0, 1, hi, dev(dx=1))
        xg_send(p, "a+", 0, 3, lo, dev(dx=3))

    def xg_relay(p):
        xg[p]["a-"].wait_recv()
        xg_send(p, "aa", 1, 2, lo, dev(dx=1))
        xg[p]["b+"].wait_recv()
        xg_send(p, "bb", 3, 2, hi, dev(dx=3))

    def xg_rest(p):
        xg[p]["b-"].wait_recv()
        xg[p]["a+"].wait_recv()

    def xg_last(p):
        xg[p]["aa"].wait_recv()
        xg[p]["bb"].wait_recv()

    osib = []

    def other_share():
        for r in (0, 2):
            for h in range(2):
                slot = other.at[0, r, h, c]
                pltpu.make_async_remote_copy(
                    src_ref=slot, dst_ref=slot, send_sem=xssem.at[0],
                    recv_sem=xrsem.at[r // 2, h], device_id=dev(dc=1), device_id_type=MESH,
                ).wait_recv()
            slot = other.at[0, r, :, c]
            osib.append(send(slot, slot, dev(dc=1)))

    def other_wait(t):
        eshare[t].wait_recv()
        if t == 0:
            for copy in osib:
                copy.wait_recv()

    gs = [None] * len(PIECES)

    def wgrad(p, r, first=False, last=False):
        q, first_col, n = PIECES[p]
        cut = pl.ds(first_col, n)
        t = 1 if q == HID else 0

        @pl.loop(0, 4)
        def _(i):
            part_kept, b = i // 2, i % 2
            h = jnp.where(part_kept == 1, yh, 1 - yh)
            rows = pl.ds(pl.multiple_of(b * 256, 256), 256)
            if r == 0:
                left = full[t, h, 2 * x + b]
            else:
                left = other[t, r - 1, h, b]
            part = tn(left, act[q, r, :, cut]) * factor

            @pl.when(part_kept == 1)
            def _():
                pre[q, rows, cut] = part if first else pre[q, rows, cut] + part

            @pl.when(part_kept == 0)
            def _():
                total = part if first else accs[rows, cut] + part
                if last:
                    gsend[q, rows, cut] = total.astype(BF)
                else:
                    accs[rows, cut] = total

        if last:
            gs[p] = send(gsend.at[q, :, cut], grecv.at[q, :, cut], dev(dyh=1))

    def shard_rows(shard):
        return pl.ds(pl.multiple_of(shard * 256, 256), 256)

    igc = [None] * 8

    def ig_other(n, m):
        shard = 2 * m + 1 - c
        igs[m] = (
            nt(act[DGATE, 0], wi[0, shard_rows(shard)]) + nt(act[DUP, 0], wi[1, shard_rows(shard)])
        ).astype(BF)
        igc[n] = send(igs.at[m], igr.at[m], dev(dc=1))

    igzc = {}

    def ig_own(n, m):
        igc[n].wait_recv()
        shard = 2 * m + c
        total = nt(act[DGATE, 0], wi[0, shard_rows(shard)]) + nt(act[DUP, 0], wi[1, shard_rows(shard)])
        igr[m] = (total + igr[m].astype(F32)).astype(BF)

    def ig_final_1():
        for copy in igzc.values():
            copy.wait_recv()
        for y in (1, 0):
            m = chip(y, 0)
            total = igr[m].astype(F32)
            for r in range(3):
                total = total + igz[r, y].astype(F32)
            if y == 1:
                igy[0] = total.astype(BF)
                igzc["y"] = send(igy.at[0], igy.at[1], dev(dyl=1))
            else:
                rowm[2], rowm[3] = total[:, :128], total[:, 128:]

    def ig_final_2():
        igzc["y"].wait_recv()
        for i in range(2):
            cols = pl.ds(i * 128, 128)
            ig_o[:, cols] = (rowm[2 + i] + igy[1, :, cols].astype(F32)).astype(BF)

    fin = 64

    def final(p):
        q, first_col, n = PIECES[p]
        cut = pl.ds(first_col, n)
        gs[p].wait_recv()
        col = row_out[...].reshape(1, h_cols) if q == HID else col_in[pl.ds(2 - q, 1), cut]

        def body(i, colmax):
            rows = pl.ds(pl.multiple_of(i * fin, fin), fin)
            g = pre[q, rows, cut] + grecv[q, rows, cut].astype(F32)
            nu = jnp.minimum(rowv[q, rows][:, :1], col) + g * g
            upd = g * lax.rsqrt(nu)
            if q == HID:
                pre[q, rows] = upd
            else:
                upd_in_o[2 - q, rows, cut] = upd.astype(BF)
            rowm[p, rows] = jnp.broadcast_to(jnp.max(nu, axis=1, keepdims=True), (fin, 128))
            return jnp.maximum(colmax, jnp.max(nu, axis=0, keepdims=True))

        colmax = lax.fori_loop(0, 512 // fin, body, jnp.zeros((1, n), F32))
        cbuf[0, pl.ds(q, 1), cut] = colmax
        rowmax = rowm[p].T[:1]
        if first_col != 0:
            rowmax = jnp.maximum(rowmax, rbuf[0, pl.ds(q, 1), pl.ds(0, 512)])
        rbuf[0, pl.ds(q, 1), pl.ds(0, 512)] = rowmax
        if q == HID:
            @pl.loop(0, h_cols // 128)
            def _(j):
                cols = pl.ds(pl.multiple_of(j * 128, 128), 128)
                upd_out_o[cols] = pre[q, :, cols].T.astype(BF)

    pl.semaphore_wait(barrier, len(peers))
    ga.start(tok_in)
    load_w = [load(w_in.at[0], wi.at[0]), load(w_in.at[1], wi.at[1])]
    cbuf[0] = jnp.zeros_like(cbuf[0])
    rbuf[0] = jnp.zeros_like(rbuf[0])
    for q in range(3):
        row = col_out[...].reshape(1, 512) if q == HID else row_in[pl.ds(2 - q, 1)]
        rowv[q] = jnp.broadcast_to(row, (128, 512)).T
    own_tok.wait()
    own_cot.wait()
    ga.one()
    gb.start(cot_in)
    load_wo = load(w_out, wo)
    ga.two()
    for copy in load_w:
        copy.wait()
    forward(0, 0, first=True)
    forward(0, 3)
    forward(0, 1)
    ga.three()
    forward(1, 0)
    ga.four()
    e2_send(0)
    forward(0, 2)
    forward(1, 3)
    forward(1, 1)
    forward(1, 2)
    make_hidden()
    xg_start(0)
    gb.one()
    load_wo.wait()
    backward(0, 0, first=True)
    gb.two()
    e2_start(0)
    backward(0, 3)
    backward(0, 1)
    gb.three()
    ge[0].one()
    backward(1, 0)
    gb.four()
    e2_send(1)
    xg_relay(0)
    ge[0].two()
    backward(0, 2)
    backward(1, 3)
    backward(1, 1)
    backward(1, 2)
    make_d()
    xg_start(1)
    e2_start(1)
    ge[0].three()
    ge[0].four()
    e2_share(0)
    other_share()
    order = [(dy, dz) for dz in (2, 1, 3, 0) for dy in (1, 0)]
    for n, (dy, dz) in enumerate(order):
        ig_other(n, chip(dy, dz))

    def ig_send(numbers):
        for n in numbers:
            dy, dz = order[n]
            ig_own(n, chip(dy, dz))
            if dz != 0:
                igzc[(dy, dz)] = send(igr.at[chip(dy, dz)], igz.at[dz - 1, dy], dev(dz=dz))

    ge[1].one()
    wgrad(0, 0, first=True)
    ig_send((0, 1))
    ge[1].two()
    ig_send((2, 3))
    ge[1].three()
    ge[1].four()
    e2_share(1)
    xg_rest(0)
    xg_last(0)
    other_wait(1)
    wgrad(0, 1)
    wgrad(0, 3)
    wgrad(0, 2, last=True)
    xg_relay(1)
    xg_start(2)
    ig_send((4, 5, 6, 7))
    other_wait(0)
    wgrad(1, 0, first=True)
    xg_rest(1)
    wgrad(1, 1)
    wgrad(1, 3)
    xg_last(1)
    wgrad(1, 2, last=True)
    wgrad(2, 0, first=True)
    xg_relay(2)
    xg_start(3)
    final(0)
    load(upd_out_o, upd_out_h)
    ig_final_1()
    xg_rest(2)
    wgrad(2, 1)
    wgrad(2, 3)
    xg_last(2)
    wgrad(2, 2, last=True)
    wgrad(3, 0, first=True)
    xg_relay(3)
    xg_rest(3)
    wgrad(3, 1)
    wgrad(3, 3)
    xg_last(3)
    wgrad(3, 2, last=True)
    ig_final_2()
    load(ig_o, ig_h)
    final(1)
    load(upd_in_o.at[1], upd_in_h.at[1])
    final(2)
    final(3)
    load(upd_in_o.at[0], upd_in_h.at[0])

    first = [
        send(rbuf.at[0], rbuf.at[1], dev(dc=1)),
        send(rbuf.at[0], rbuf.at[2], dev(dyl=1)),
        send(rbuf.at[0], rbuf.at[3], dev(dyl=1, dc=1)),
        send(cbuf.at[0], cbuf.at[1], dev(dyh=1)),
    ]
    for copy in first:
        copy.wait_recv()
    rbuf[4] = jnp.maximum(jnp.maximum(rbuf[0], rbuf[1]), jnp.maximum(rbuf[2], rbuf[3]))
    cbuf[2] = jnp.maximum(cbuf[0], cbuf[1])
    second = []
    for r in range(1, 4):
        second.append(send(rbuf.at[4], rbuf.at[4 + r], dev(dz=r)))
        second.append(send(cbuf.at[2], cbuf.at[2 + r], dev(dx=r)))
    for copy in second:
        copy.wait_recv()
    rmax_o[...] = jnp.maximum(jnp.maximum(rbuf[4], rbuf[5]), jnp.maximum(rbuf[6], rbuf[7]))
    cmax_o[...] = jnp.maximum(jnp.maximum(cbuf[2], cbuf[3]), jnp.maximum(cbuf[4], cbuf[5]))

    for copy in loads[5:]:
        copy.wait()
    for copy in sent[-SENDING:]:
        copy.wait_send()
    for taken, copy in xsent:
        @pl.when(taken)
        def _(copy=copy):
            copy.wait_send()


def finish(
    ig, upd_in, upd_out, rmax, cmax,
    ig_o, upd_in_o, upd_out_o, row_in_o, col_in_o, row_out_o, col_out_o,
    ig_v, upd_in_v, upd_out_v, sem,
):
    steps = ((ig, ig_v, ig_o), (upd_in, upd_in_v, upd_in_o), (upd_out, upd_out_v, upd_out_o))
    ins = [pltpu.make_async_copy(s, v, sem.at[0, i]) for i, (s, v, o) in enumerate(steps)]
    copies = [pltpu.make_async_copy(v, o, sem.at[1, i]) for i, (s, v, o) in enumerate(steps)]
    for copy in ins:
        copy.start()
    n = row_in_o.shape[1]
    col_out_o[...] = rmax[HID, pl.ds(0, n)]
    row_out_o[...] = cmax[HID]
    for q in (DUP, DGATE):
        row_in_o[pl.ds(2 - q, 1)] = rmax[q : q + 1, :n]
        col_in_o[pl.ds(2 - q, 1)] = cmax[q : q + 1]
    for before, copy in zip(ins, copies):
        before.wait()
        copy.start()
    for copy in copies:
        copy.wait()


def local(tokens, cotangent, w_in, w_out, row_in, col_in, row_out, col_out):
    t_rows, d_cols = tokens.shape
    h_cols = w_out.shape[0]
    factor = 1.0 / math.sqrt(t_rows * lax.axis_size("dp"))
    vmem = pl.BlockSpec(memory_space=pltpu.VMEM)
    hbm = pl.BlockSpec(memory_space=pl.ANY)
    shapes = (
        jax.ShapeDtypeStruct((t_rows, 256), BF),
        jax.ShapeDtypeStruct((2, 512, h_cols), BF),
        jax.ShapeDtypeStruct((h_cols, 512), BF),
        jax.ShapeDtypeStruct((8, h_cols), F32),
        jax.ShapeDtypeStruct((8, h_cols), F32),
    )
    out = pl.pallas_call(
        functools.partial(kernel, factor),
        out_shape=shapes,
        in_specs=[hbm] * 4 + [vmem] * 4,
        out_specs=[hbm] * 3 + [vmem] * 2,
        scratch_shapes=[
            pltpu.VMEM((2, 2, 8, t_rows, 256), BF),
            pltpu.VMEM(w_in.shape, BF),
            pltpu.VMEM(w_out.shape, BF),
            pltpu.VMEM((3, t_rows, h_cols), F32),
            pltpu.VMEM((3, 4, t_rows, h_cols), BF),
            pltpu.VMEM((2, 3, 2, 2, t_rows, 256), BF),
            pltpu.VMEM((512, h_cols), F32),
            pltpu.VMEM((3, 512, h_cols), BF),
            pltpu.VMEM((3, 512, h_cols), BF),
            pltpu.VMEM((8, t_rows, 256), BF),
            pltpu.VMEM((8, t_rows, 256), BF),
            pltpu.VMEM((3, 2, t_rows, 256), BF),
            pltpu.VMEM((2, t_rows, 256), BF),
            pltpu.VMEM((3, 512, 128), F32),
            pltpu.VMEM((4, 512, 128), F32),
            pltpu.VMEM((8, 8, h_cols), F32),
            pltpu.VMEM((6, 8, h_cols), F32),
        ]
        + [pltpu.VMEM(s.shape, BF) for s in shapes[:3]]
        + [
            pltpu.SemaphoreType.DMA((9,)),
            pltpu.SemaphoreType.DMA((SENDING,)),
            pltpu.SemaphoreType.DMA((MESSAGES,)),
            pltpu.SemaphoreType.DMA((8,)),
            pltpu.SemaphoreType.DMA((2, 2)),
        ],
        compiler_params=pltpu.CompilerParams(
            collective_id=0, has_side_effects=True, vmem_limit_bytes=62 * 2**20
        ),
        cost_estimate=pl.CostEstimate(
            flops=21_500_000_000, bytes_accessed=22_000_000, transcendentals=330_000
        ),
    )(tokens, cotangent, w_in, w_out, row_in, col_in, row_out, col_out)
    return pl.pallas_call(
        finish,
        out_shape=shapes[:3]
        + (
            jax.ShapeDtypeStruct(row_in.shape, F32),
            jax.ShapeDtypeStruct(col_in.shape, F32),
            jax.ShapeDtypeStruct(row_out.shape, F32),
            jax.ShapeDtypeStruct(col_out.shape, F32),
        ),
        in_specs=[hbm] * 3 + [vmem] * 2,
        out_specs=[hbm] * 3 + [vmem] * 4,
        scratch_shapes=[pltpu.VMEM(s.shape, BF) for s in shapes[:3]]
        + [pltpu.SemaphoreType.DMA((2, 3))],
    )(*out)


def solution(mesh):
    return jax.shard_map(
        local,
        mesh=mesh,
        in_specs=(
            P("dp", "mp"),
            P("dp", "mp"),
            P(None, None, "mp"),
            P("mp", None),
            P(None, "dp"),
            P(None, "mp"),
            P("mp"),
            P("dp"),
        ),
        out_specs=(
            P("dp", "mp"),
            P(None, "dp", "mp"),
            P("mp", "dp"),
            P(None, "dp"),
            P(None, "mp"),
            P("mp"),
            P("dp"),
        ),
        check_vma=False,
    )
```

```python
import functools
import math

import jax
import jax.numpy as jnp
from jax import lax
from jax.experimental import pallas as pl
from jax.experimental.pallas import tpu as pltpu
from jax.sharding import PartitionSpec as P

BF = jnp.bfloat16
F32 = jnp.float32
MESH = pl.DeviceIdType.MESH
ROOT = math.sqrt(2.0 / math.pi)

HID, DUP, DGATE = 0, 1, 2
MESSAGES = 133
SENDING = 48
PIECES = ((HID, 0, 640), (DUP, 0, 640), (DGATE, 0, 384), (DGATE, 384, 256))


def nn(a, b):
    return jnp.dot(a, b, preferred_element_type=F32)


def nt(a, b):
    return lax.dot_general(a, b, (((1,), (1,)), ((), ())), preferred_element_type=F32)


def tn(a, b):
    return lax.dot_general(a, b, (((0,), (0,)), ((), ())), preferred_element_type=F32)


def kernel(
    factor,
    tok_in,
    cot_in,
    w_in,
    w_out,
    row_in,
    col_in,
    row_out,
    col_out,
    ig_h,
    upd_in_h,
    upd_out_h,
    rmax_o,
    cmax_o,
    full,
    wi,
    wo,
    pre,
    own,
    act,
    kept,
    other,
    accs,
    gsend,
    grecv,
    igs,
    igr,
    igz,
    igy,
    colv,
    rbuf,
    cbuf,
    ig_o,
    upd_in_o,
    upd_out_o,
    lsem,
    ssem,
    rsem,
    xssem,
    xrsem,
):
    dp, mp = lax.axis_index("dp"), lax.axis_index("mp")
    yh, x = dp // 4, dp % 4
    yl, z, c = mp // 8, (mp // 2) % 4, mp % 2
    t_rows, h_cols = pre.shape[1], pre.shape[2]
    half = t_rows // 2

    def dev(dx=0, dyh=0, dyl=0, dz=0, dc=0):
        return (
            lax.rem(yh + dyh, 2) * 4 + lax.rem(x + dx, 4),
            lax.rem(yl + dyl, 2) * 8 + lax.rem(z + dz, 4) * 2 + lax.rem(c + dc, 2),
        )

    def chip(dy, dz):
        return lax.rem(yl + dy, 2) * 4 + lax.rem(z + dz, 4)

    peers = [
        dev(dz=1), dev(dz=3), dev(dz=2), dev(dyl=1), dev(dc=1), dev(dyl=1, dc=1),
        dev(dx=1), dev(dx=3), dev(dx=2), dev(dyh=1),
    ]
    barrier = pltpu.get_barrier_semaphore()
    for peer in peers:
        pl.semaphore_signal(barrier, inc=1, device_id=peer, device_id_type=MESH)

    loads = []

    def load(src, dst):
        copy = pltpu.make_async_copy(src, dst, lsem.at[len(loads)])
        copy.start()
        loads.append(copy)
        return copy

    own_tok = load(tok_in, full.at[0, yl, z * 2 + c])
    own_cot = load(cot_in, full.at[1, yl, z * 2 + c])

    sent = []

    def send(src, dst, device):
        i = len(sent)
        if i >= SENDING:
            sent[i - SENDING].wait_send()
        copy = pltpu.make_async_remote_copy(
            src_ref=src, dst_ref=dst, send_sem=ssem.at[i % SENDING], recv_sem=rsem.at[i],
            device_id=device, device_id_type=MESH,
        )
        copy.start()
        sent.append(copy)
        return copy

    xsent = []

    def xsend(dy, dz, src):
        origin_z = lax.rem(z + dz, 4)
        origin_y = lax.rem(yl + dy, 2)
        dx = lax.rem(origin_z + 4 - x, 4)
        there = dx // 2 * 2
        i = len(xsent)
        copy = pltpu.make_async_remote_copy(
            src_ref=src,
            dst_ref=other.at[0, there, origin_y, c],
            send_sem=xssem.at[i], recv_sem=xrsem.at[there // 2, origin_y],
            device_id=(yh * 4 + origin_z, mp), device_id_type=MESH,
        )
        xsent.append((dx % 2 == 1, copy))

        @pl.when(dx % 2 == 1)
        def _():
            copy.start()

    sib = [{}, {}]

    class Gather:
        def __init__(self, slot, share):
            self.slot, self.share, self.got = slot, share, {}

        def push(self, name, dy, dz, part, device, src=None):
            slot = self.slot(dy, dz, part)
            self.got[name] = send(slot if src is None else self.part_of(src, part), slot, device)

        def part_of(self, src, part):
            n = src.shape[0] // 2
            return src.at[pl.ds(part * n, n)]

        def wait(self, name):
            self.got[name].wait_recv()

        def start(self, src=None):
            self.push("z-0", 0, 0, 0, dev(dz=1), src)
            self.push("z+1", 0, 0, 1, dev(dz=3), src)
            self.push("y0", 0, 0, 0, dev(dyl=1), src)
            self.push("z-1", 0, 0, 1, dev(dz=1), src)
            self.push("z+0", 0, 0, 0, dev(dz=3), src)
            self.push("y1", 0, 0, 1, dev(dyl=1), src)
            self.share(0, 0, src)

        def one(self):
            self.wait("z-0")
            self.push("zz0", 0, 3, 0, dev(dz=1))
            self.wait("z+1")
            self.push("zz1", 0, 1, 1, dev(dz=3))
            self.wait("y0")
            self.push("yz-0", 1, 0, 0, dev(dz=1))
            self.push("yz+0", 1, 0, 0, dev(dz=3))
            self.wait("z-1")
            self.share(0, 3, None)
            self.wait("z+0")
            self.share(0, 1, None)
            self.wait("y1")
            self.push("yz-1", 1, 0, 1, dev(dz=1))
            self.push("yz+1", 1, 0, 1, dev(dz=3))
            self.share(1, 0, None)

        def two(self):
            self.wait("zz0")
            self.push("yzz0", 0, 2, 0, dev(dyl=1))
            self.wait("zz1")
            self.push("yzz1", 0, 2, 1, dev(dyl=1))
            self.share(0, 2, None)

        def three(self):
            self.wait("yz-0")
            self.wait("yz-1")
            self.share(1, 3, None)
            self.wait("yz+0")
            self.wait("yz+1")
            self.share(1, 1, None)

        def four(self):
            self.wait("yzz0")
            self.wait("yzz1")
            self.share(1, 2, None)

    def full_gather(t):
        def slot(dy, dz, part):
            ref = full.at[t, lax.rem(yl + dy, 2), lax.rem(z + dz, 4) * 2 + c]
            return ref if part is None else ref.at[pl.ds(part * half, half)]

        def share(dy, dz, src):
            ref = slot(dy, dz, None)
            sib[t][(dy, dz)] = send(ref if src is None else src, ref, dev(dc=1))
            if t == 0:
                xsend(dy, dz, ref if src is None else src)

        return Gather(slot, share)

    e2_rows = t_rows // 8
    far = ((1, 1), (0, 3))

    def e2_gather(t):
        first, count = far[t]

        def slot(dy, dz, part):
            n = e2_rows // 2
            rows = pl.ds(pl.multiple_of(chip(dy, dz) * e2_rows + part * n, n), n)
            return other.at[t, pl.ds(first, count), :, c, rows]

        return Gather(slot, lambda dy, dz, src: None)

    ga, gb = full_gather(0), full_gather(1)
    ge = [e2_gather(0), e2_gather(1)]
    e2 = [[], []]
    eshare = [None, None]

    def e2_send(t):
        rows = pl.ds(pl.multiple_of(chip(0, 0) * e2_rows, e2_rows), e2_rows)
        first, count = far[t]
        for r in range(first, first + count):
            e2[t].append(
                send(
                    full.at[t, :, lax.rem(x + r + 1, 4) * 2 + c, rows],
                    other.at[t, r, :, c, rows],
                    dev(dx=r + 1),
                )
            )

    def e2_start(t):
        for copy in e2[t]:
            copy.wait_recv()
        ge[t].start()

    def e2_share(t):
        first, count = far[t]
        slot = other.at[t, pl.ds(first, count), :, c]
        eshare[t] = send(slot, slot, dev(dc=1))

    def forward(dy, dz, first=False):
        sib[0][(dy, dz)].wait_recv()
        m = chip(dy, dz)
        my, mz = lax.rem(yl + dy, 2), lax.rem(z + dz, 4) * 2

        @pl.loop(0, 4)
        def _(i):
            k, rows = i // 2, pl.ds(pl.multiple_of((i % 2) * half, half), half)
            part = nn(full[0, my, mz, rows], wi[k, pl.ds(pl.multiple_of(m * 512, 512), 256)]) + nn(
                full[0, my, mz + 1, rows], wi[k, pl.ds(pl.multiple_of(m * 512 + 256, 256), 256)]
            )
            if first:
                pre[k, rows] = part
            else:
                pre[k, rows] += part

    def backward(dy, dz, first=False):
        sib[1][(dy, dz)].wait_recv()
        m = chip(dy, dz)
        my, mz = lax.rem(yl + dy, 2), lax.rem(z + dz, 4) * 2

        @pl.loop(0, 2)
        def _(i):
            rows = pl.ds(pl.multiple_of(i * half, half), half)
            part = nt(full[1, my, mz, rows], wo[:, pl.ds(pl.multiple_of(m * 512, 512), 256)]) + nt(
                full[1, my, mz + 1, rows], wo[:, pl.ds(pl.multiple_of(m * 512 + 256, 256), 256)]
            )
            if first:
                pre[2, rows] = part
            else:
                pre[2, rows] += part

    def blocks(body):
        n = h_cols // 128

        @pl.loop(0, (t_rows // 128) * n)
        def _(i):
            body(
                pl.ds(pl.multiple_of(i // n * 128, 128), 128),
                pl.ds(pl.multiple_of(lax.rem(i, n) * 128, 128), 128),
            )

    def make_hidden():
        def body(rows, cols):
            v = pre[0, rows, cols]
            up = pre[1, rows, cols]
            t = jnp.tanh(ROOT * (v + 0.044715 * v * v * v))
            activated = 0.5 * v * (1.0 + t)
            slopes = 0.5 * (1.0 + t) + 0.5 * v * (1.0 - t * t) * ROOT * (
                1.0 + 3.0 * 0.044715 * v * v
            )
            act[HID, 0, cols, rows] = (activated * up).T.astype(BF)
            pre[0, rows, cols] = activated
            pre[1, rows, cols] = up * slopes

        blocks(body)

    def make_d():
        def body(rows, cols):
            d = pre[2, rows, cols]
            for i in range(2):
                value = d * pre[i, rows, cols]
                own[i, rows, cols] = value.astype(BF)
                act[DUP + i, 0, cols, rows] = value.T.astype(BF)

        blocks(body)

    xg = [{} for _ in PIECES]
    lo, hi = 0, 1

    def xg_send(p, name, source, there, part, device):
        q, first_unit, units = PIECES[p]
        cut = pl.ds(first_unit + part * (units // 2), units // 2)
        xg[p][name] = send(act.at[q, source, cut], act.at[q, there, cut], device)

    def xg_start(p):
        xg_send(p, "a-", 0, 1, lo, dev(dx=1))
        xg_send(p, "b+", 0, 3, hi, dev(dx=3))
        xg_send(p, "b-", 0, 1, hi, dev(dx=1))
        xg_send(p, "a+", 0, 3, lo, dev(dx=3))

    def xg_relay(p):
        xg[p]["a-"].wait_recv()
        xg_send(p, "aa", 1, 2, lo, dev(dx=1))
        xg[p]["b+"].wait_recv()
        xg_send(p, "bb", 3, 2, hi, dev(dx=3))

    def xg_rest(p):
        xg[p]["b-"].wait_recv()
        xg[p]["a+"].wait_recv()

    def xg_last(p):
        xg[p]["aa"].wait_recv()
        xg[p]["bb"].wait_recv()

    osib = []

    def other_share():
        for r in (0, 2):
            for h in range(2):
                slot = other.at[0, r, h, c]
                pltpu.make_async_remote_copy(
                    src_ref=slot, dst_ref=slot, send_sem=xssem.at[0],
                    recv_sem=xrsem.at[r // 2, h], device_id=dev(dc=1), device_id_type=MESH,
                ).wait_recv()
            slot = other.at[0, r, :, c]
            osib.append(send(slot, slot, dev(dc=1)))

    def other_wait(t):
        eshare[t].wait_recv()
        if t == 0:
            for copy in osib:
                copy.wait_recv()

    gs = [None] * len(PIECES)

    def wgrad(p, r, first=False, last=False):
        q, first_unit, n = PIECES[p]
        cut = pl.ds(first_unit, n)
        t = 1 if q == HID else 0

        @pl.loop(0, 4)
        def _(i):
            part_kept, b = i // 2, i % 2
            h = jnp.where(part_kept == 1, yh, 1 - yh)
            cols = pl.ds(pl.multiple_of(b * 256, 256), 256)
            if r == 0:
                right = full[t, h, 2 * x + b]
            else:
                right = other[t, r - 1, h, b]
            part = nn(act[q, r, cut], right) * factor

            @pl.when(part_kept == 1)
            def _():
                kept[q, cut, cols] = part if first else kept[q, cut, cols] + part

            @pl.when(part_kept == 0)
            def _():
                total = part if first else accs[cut, cols] + part
                if last:
                    gsend[q, cut, cols] = total.astype(BF)
                else:
                    accs[cut, cols] = total

        if last:
            gs[p] = send(gsend.at[q, cut], grecv.at[q, cut], dev(dyh=1))

    def shard_rows(shard):
        return pl.ds(pl.multiple_of(shard * 256, 256), 256)

    igc = [None] * 8

    def ig_other(n, m):
        shard = 2 * m + 1 - c
        igs[m] = (
            nt(own[1], wi[0, shard_rows(shard)]) + nt(own[0], wi[1, shard_rows(shard)])
        ).astype(BF)
        igc[n] = send(igs.at[m], igr.at[m], dev(dc=1))

    igzc = {}

    def ig_own(n, m):
        igc[n].wait_recv()
        shard = 2 * m + c
        total = nt(own[1], wi[0, shard_rows(shard)]) + nt(own[0], wi[1, shard_rows(shard)])
        igr[m] = (total + igr[m].astype(F32)).astype(BF)

    def ig_final_1():
        for copy in igzc.values():
            copy.wait_recv()
        for y in (1, 0):
            m = chip(y, 0)
            total = igr[m].astype(F32)
            for r in range(3):
                total = total + igz[r, y].astype(F32)
            if y == 1:
                igy[0] = total.astype(BF)
                igzc["y"] = send(igy.at[0], igy.at[1], dev(dyl=1))
            else:
                pre[0, :, pl.ds(0, 256)] = total

    def ig_final_2():
        igzc["y"].wait_recv()
        ig_o[...] = (pre[0, :, pl.ds(0, 256)] + igy[1].astype(F32)).astype(BF)

    fin = 128

    def final(p):
        q, first_unit, n = PIECES[p]
        gs[p].wait_recv()
        row = col_out[...].reshape(1, 512) if q == HID else row_in[pl.ds(2 - q, 1)]

        def body(i, rowmax):
            units = pl.ds(pl.multiple_of(first_unit + i * fin, fin), fin)
            g = kept[q, units] + grecv[q, units].astype(F32)
            nu = jnp.minimum(colv[q, units][:, :1], row) + g * g
            upd = g * lax.rsqrt(nu)
            if q == HID:
                upd_out_o[units] = upd.astype(BF)
            else:
                upd_in_o[2 - q, :, units] = upd.T.astype(BF)
            colv[q, units] = jnp.broadcast_to(jnp.max(nu, axis=1, keepdims=True), (fin, 128))
            return jnp.maximum(rowmax, jnp.max(nu, axis=0, keepdims=True))

        rowmax = lax.fori_loop(0, n // fin, body, jnp.zeros((1, 512), F32))
        cut = pl.ds(first_unit, n)
        cbuf[0, pl.ds(q, 1), cut] = colv[q, cut].T[:1]
        if first_unit != 0:
            rowmax = jnp.maximum(rowmax, rbuf[0, pl.ds(q, 1), pl.ds(0, 512)])
        rbuf[0, pl.ds(q, 1), pl.ds(0, 512)] = rowmax

    pl.semaphore_wait(barrier, len(peers))
    ga.start(tok_in)
    load_w = [load(w_in.at[0], wi.at[0]), load(w_in.at[1], wi.at[1])]
    cbuf[0] = jnp.zeros_like(cbuf[0])
    rbuf[0] = jnp.zeros_like(rbuf[0])
    for q in range(3):
        col = row_out[...].reshape(1, h_cols) if q == HID else col_in[pl.ds(2 - q, 1)]
        colv[q] = jnp.broadcast_to(col, (128, h_cols)).T
    own_tok.wait()
    own_cot.wait()
    ga.one()
    gb.start(cot_in)
    load_wo = load(w_out, wo)
    ga.two()
    for copy in load_w:
        copy.wait()
    forward(0, 0, first=True)
    forward(0, 3)
    forward(0, 1)
    ga.three()
    forward(1, 0)
    ga.four()
    e2_send(0)
    forward(0, 2)
    forward(1, 3)
    forward(1, 1)
    forward(1, 2)
    make_hidden()
    xg_start(0)
    gb.one()
    load_wo.wait()
    backward(0, 0, first=True)
    gb.two()
    e2_start(0)
    backward(0, 3)
    backward(0, 1)
    gb.three()
    ge[0].one()
    backward(1, 0)
    gb.four()
    e2_send(1)
    xg_relay(0)
    ge[0].two()
    backward(0, 2)
    backward(1, 3)
    backward(1, 1)
    backward(1, 2)
    make_d()
    xg_start(1)
    e2_start(1)
    ge[0].three()
    ge[0].four()
    e2_share(0)
    other_share()
    order = [(dy, dz) for dz in (2, 1, 3, 0) for dy in (1, 0)]
    for n, (dy, dz) in enumerate(order):
        ig_other(n, chip(dy, dz))

    def ig_send(numbers):
        for n in numbers:
            dy, dz = order[n]
            ig_own(n, chip(dy, dz))
            if dz != 0:
                igzc[(dy, dz)] = send(igr.at[chip(dy, dz)], igz.at[dz - 1, dy], dev(dz=dz))

    ge[1].one()
    wgrad(0, 0, first=True)
    ig_send((0, 1))
    ge[1].two()
    ig_send((2, 3))
    ge[1].three()
    ge[1].four()
    e2_share(1)
    xg_rest(0)
    xg_last(0)
    other_wait(1)
    wgrad(0, 1)
    wgrad(0, 3)
    wgrad(0, 2, last=True)
    xg_relay(1)
    xg_start(2)
    ig_send((4, 5, 6, 7))
    other_wait(0)
    wgrad(1, 0, first=True)
    xg_rest(1)
    wgrad(1, 1)
    wgrad(1, 3)
    xg_last(1)
    wgrad(1, 2, last=True)
    wgrad(2, 0, first=True)
    xg_relay(2)
    xg_start(3)
    final(0)
    load(upd_out_o, upd_out_h)
    ig_final_1()
    xg_rest(2)
    wgrad(2, 1)
    wgrad(2, 3)
    xg_last(2)
    wgrad(2, 2, last=True)
    wgrad(3, 0, first=True)
    xg_relay(3)
    xg_rest(3)
    wgrad(3, 1)
    wgrad(3, 3)
    xg_last(3)
    wgrad(3, 2, last=True)
    ig_final_2()
    load(ig_o, ig_h)
    final(1)
    load(upd_in_o.at[1], upd_in_h.at[1])
    final(2)
    final(3)
    load(upd_in_o.at[0], upd_in_h.at[0])

    first = [
        send(rbuf.at[0], rbuf.at[1], dev(dc=1)),
        send(rbuf.at[0], rbuf.at[2], dev(dyl=1)),
        send(rbuf.at[0], rbuf.at[3], dev(dyl=1, dc=1)),
        send(cbuf.at[0], cbuf.at[1], dev(dyh=1)),
    ]
    for copy in first:
        copy.wait_recv()
    rbuf[4] = jnp.maximum(jnp.maximum(rbuf[0], rbuf[1]), jnp.maximum(rbuf[2], rbuf[3]))
    cbuf[2] = jnp.maximum(cbuf[0], cbuf[1])
    second = []
    for r in range(1, 4):
        second.append(send(rbuf.at[4], rbuf.at[4 + r], dev(dz=r)))
        second.append(send(cbuf.at[2], cbuf.at[2 + r], dev(dx=r)))
    for copy in second:
        copy.wait_recv()
    rmax_o[...] = jnp.maximum(jnp.maximum(rbuf[4], rbuf[5]), jnp.maximum(rbuf[6], rbuf[7]))
    cmax_o[...] = jnp.maximum(jnp.maximum(cbuf[2], cbuf[3]), jnp.maximum(cbuf[4], cbuf[5]))

    for copy in loads[5:]:
        copy.wait()
    for copy in sent[-SENDING:]:
        copy.wait_send()
    for taken, copy in xsent:
        @pl.when(taken)
        def _(copy=copy):
            copy.wait_send()


def finish(
    ig, upd_in, upd_out, rmax, cmax,
    ig_o, upd_in_o, upd_out_o, row_in_o, col_in_o, row_out_o, col_out_o,
    ig_v, upd_in_v, upd_out_v, sem,
):
    steps = ((ig, ig_v, ig_o), (upd_in, upd_in_v, upd_in_o), (upd_out, upd_out_v, upd_out_o))
    ins = [pltpu.make_async_copy(s, v, sem.at[0, i]) for i, (s, v, o) in enumerate(steps)]
    copies = [pltpu.make_async_copy(v, o, sem.at[1, i]) for i, (s, v, o) in enumerate(steps)]
    for copy in ins:
        copy.start()
    n = row_in_o.shape[1]
    col_out_o[...] = rmax[HID, pl.ds(0, n)]
    row_out_o[...] = cmax[HID]
    for q in (DUP, DGATE):
        row_in_o[pl.ds(2 - q, 1)] = rmax[q : q + 1, :n]
        col_in_o[pl.ds(2 - q, 1)] = cmax[q : q + 1]
    for before, copy in zip(ins, copies):
        before.wait()
        copy.start()
    for copy in copies:
        copy.wait()


def local(tokens, cotangent, w_in, w_out, row_in, col_in, row_out, col_out):
    t_rows, d_cols = tokens.shape
    h_cols = w_out.shape[0]
    factor = 1.0 / math.sqrt(t_rows * lax.axis_size("dp"))
    vmem = pl.BlockSpec(memory_space=pltpu.VMEM)
    hbm = pl.BlockSpec(memory_space=pl.ANY)
    shapes = (
        jax.ShapeDtypeStruct((t_rows, 256), BF),
        jax.ShapeDtypeStruct((2, 512, h_cols), BF),
        jax.ShapeDtypeStruct((h_cols, 512), BF),
        jax.ShapeDtypeStruct((8, h_cols), F32),
        jax.ShapeDtypeStruct((8, h_cols), F32),
    )
    out = pl.pallas_call(
        functools.partial(kernel, factor),
        out_shape=shapes,
        in_specs=[hbm] * 4 + [vmem] * 4,
        out_specs=[hbm] * 3 + [vmem] * 2,
        scratch_shapes=[
            pltpu.VMEM((2, 2, 8, t_rows, 256), BF),
            pltpu.VMEM(w_in.shape, BF),
            pltpu.VMEM(w_out.shape, BF),
            pltpu.VMEM((3, t_rows, h_cols), F32),
            pltpu.VMEM((2, t_rows, h_cols), BF),
            pltpu.VMEM((3, 4, h_cols, t_rows), BF),
            pltpu.VMEM((3, h_cols, 512), F32),
            pltpu.VMEM((2, 3, 2, 2, t_rows, 256), BF),
            pltpu.VMEM((h_cols, 512), F32),
            pltpu.VMEM((3, h_cols, 512), BF),
            pltpu.VMEM((3, h_cols, 512), BF),
            pltpu.VMEM((8, t_rows, 256), BF),
            pltpu.VMEM((8, t_rows, 256), BF),
            pltpu.VMEM((3, 2, t_rows, 256), BF),
            pltpu.VMEM((2, t_rows, 256), BF),
            pltpu.VMEM((3, h_cols, 128), F32),
            pltpu.VMEM((8, 8, h_cols), F32),
            pltpu.VMEM((6, 8, h_cols), F32),
        ]
        + [pltpu.VMEM(s.shape, BF) for s in shapes[:3]]
        + [
            pltpu.SemaphoreType.DMA((9,)),
            pltpu.SemaphoreType.DMA((SENDING,)),
            pltpu.SemaphoreType.DMA((MESSAGES,)),
            pltpu.SemaphoreType.DMA((8,)),
            pltpu.SemaphoreType.DMA((2, 2)),
        ],
        compiler_params=pltpu.CompilerParams(
            collective_id=0, has_side_effects=True, vmem_limit_bytes=62 * 2**20
        ),
        cost_estimate=pl.CostEstimate(
            flops=21_500_000_000, bytes_accessed=22_000_000, transcendentals=330_000
        ),
    )(tokens, cotangent, w_in, w_out, row_in, col_in, row_out, col_out)
    return pl.pallas_call(
        finish,
        out_shape=shapes[:3]
        + (
            jax.ShapeDtypeStruct(row_in.shape, F32),
            jax.ShapeDtypeStruct(col_in.shape, F32),
            jax.ShapeDtypeStruct(row_out.shape, F32),
            jax.ShapeDtypeStruct(col_out.shape, F32),
        ),
        in_specs=[hbm] * 3 + [vmem] * 2,
        out_specs=[hbm] * 3 + [vmem] * 4,
        scratch_shapes=[pltpu.VMEM(s.shape, BF) for s in shapes[:3]]
        + [pltpu.SemaphoreType.DMA((2, 3))],
    )(*out)


def solution(mesh):
    return jax.shard_map(
        local,
        mesh=mesh,
        in_specs=(
            P("dp", "mp"),
            P("dp", "mp"),
            P(None, None, "mp"),
            P("mp", None),
            P(None, "dp"),
            P(None, "mp"),
            P("mp"),
            P("dp"),
        ),
        out_specs=(
            P("dp", "mp"),
            P(None, "dp", "mp"),
            P("mp", "dp"),
            P(None, "dp"),
            P(None, "mp"),
            P("mp"),
            P("dp"),
        ),
        check_vma=False,
    )
```

```python
import functools
import math

import jax
import jax.numpy as jnp
from jax import lax
from jax.experimental import pallas as pl
from jax.experimental.pallas import tpu as pltpu
from jax.sharding import PartitionSpec as P

BF = jnp.bfloat16
F32 = jnp.float32
MESH = pl.DeviceIdType.MESH
ROOT = math.sqrt(2.0 / math.pi)

HID, DUP, DGATE = 0, 1, 2
MESSAGES = 133
SENDING = 48
PIECES = ((HID, 0, 640), (DUP, 0, 640), (DGATE, 0, 384), (DGATE, 384, 256))


def nn(a, b):
    return jnp.dot(a, b, preferred_element_type=F32)


def nt(a, b):
    return lax.dot_general(a, b, (((1,), (1,)), ((), ())), preferred_element_type=F32)


def tn(a, b):
    return lax.dot_general(a, b, (((0,), (0,)), ((), ())), preferred_element_type=F32)


def kernel(
    factor,
    tok_in,
    cot_in,
    w_in,
    w_out,
    row_in,
    col_in,
    row_out,
    col_out,
    ig_h,
    upd_in_h,
    upd_out_h,
    rmax_o,
    cmax_o,
    full,
    wi,
    wo,
    pre,
    act,
    other,
    accs,
    gsend,
    grecv,
    igs,
    igr,
    igz,
    igy,
    rowv,
    rowm,
    rbuf,
    cbuf,
    ig_o,
    upd_in_o,
    upd_out_o,
    lsem,
    ssem,
    rsem,
    xssem,
    xrsem,
):
    dp, mp = lax.axis_index("dp"), lax.axis_index("mp")
    yh, x = dp // 4, dp % 4
    yl, z, c = mp // 8, (mp // 2) % 4, mp % 2
    t_rows, h_cols = pre.shape[1], pre.shape[2]
    half = t_rows // 2

    def dev(dx=0, dyh=0, dyl=0, dz=0, dc=0):
        return (
            lax.rem(yh + dyh, 2) * 4 + lax.rem(x + dx, 4),
            lax.rem(yl + dyl, 2) * 8 + lax.rem(z + dz, 4) * 2 + lax.rem(c + dc, 2),
        )

    def chip(dy, dz):
        return lax.rem(yl + dy, 2) * 4 + lax.rem(z + dz, 4)

    peers = [
        dev(dz=1), dev(dz=3), dev(dz=2), dev(dyl=1), dev(dc=1), dev(dyl=1, dc=1),
        dev(dx=1), dev(dx=3), dev(dx=2), dev(dyh=1),
    ]
    barrier = pltpu.get_barrier_semaphore()
    for peer in peers:
        pl.semaphore_signal(barrier, inc=1, device_id=peer, device_id_type=MESH)

    loads = []

    def load(src, dst):
        copy = pltpu.make_async_copy(src, dst, lsem.at[len(loads)])
        copy.start()
        loads.append(copy)
        return copy

    own_tok = load(tok_in, full.at[0, yl, z * 2 + c])
    own_cot = load(cot_in, full.at[1, yl, z * 2 + c])

    sent = []

    def send(src, dst, device):
        i = len(sent)
        if i >= SENDING:
            sent[i - SENDING].wait_send()
        copy = pltpu.make_async_remote_copy(
            src_ref=src, dst_ref=dst, send_sem=ssem.at[i % SENDING], recv_sem=rsem.at[i],
            device_id=device, device_id_type=MESH,
        )
        copy.start()
        sent.append(copy)
        return copy

    xsent = []

    def xsend(dy, dz, src):
        origin_z = lax.rem(z + dz, 4)
        origin_y = lax.rem(yl + dy, 2)
        dx = lax.rem(origin_z + 4 - x, 4)
        there = dx // 2 * 2
        i = len(xsent)
        copy = pltpu.make_async_remote_copy(
            src_ref=src,
            dst_ref=other.at[0, there, origin_y, c],
            send_sem=xssem.at[i], recv_sem=xrsem.at[there // 2, origin_y],
            device_id=(yh * 4 + origin_z, mp), device_id_type=MESH,
        )
        xsent.append((dx % 2 == 1, copy))

        @pl.when(dx % 2 == 1)
        def _():
            copy.start()

    sib = [{}, {}]

    class Gather:
        def __init__(self, slot, share):
            self.slot, self.share, self.got = slot, share, {}

        def push(self, name, dy, dz, part, device, src=None):
            slot = self.slot(dy, dz, part)
            self.got[name] = send(slot if src is None else self.part_of(src, part), slot, device)

        def part_of(self, src, part):
            n = src.shape[0] // 2
            return src.at[pl.ds(part * n, n)]

        def wait(self, name):
            self.got[name].wait_recv()

        def start(self, src=None):
            self.push("z-0", 0, 0, 0, dev(dz=1), src)
            self.push("z+1", 0, 0, 1, dev(dz=3), src)
            self.push("y0", 0, 0, 0, dev(dyl=1), src)
            self.push("z-1", 0, 0, 1, dev(dz=1), src)
            self.push("z+0", 0, 0, 0, dev(dz=3), src)
            self.push("y1", 0, 0, 1, dev(dyl=1), src)
            self.share(0, 0, src)

        def one(self):
            self.wait("z-0")
            self.push("zz0", 0, 3, 0, dev(dz=1))
            self.wait("z+1")
            self.push("zz1", 0, 1, 1, dev(dz=3))
            self.wait("y0")
            self.push("yz-0", 1, 0, 0, dev(dz=1))
            self.push("yz+0", 1, 0, 0, dev(dz=3))
            self.wait("z-1")
            self.share(0, 3, None)
            self.wait("z+0")
            self.share(0, 1, None)
            self.wait("y1")
            self.push("yz-1", 1, 0, 1, dev(dz=1))
            self.push("yz+1", 1, 0, 1, dev(dz=3))
            self.share(1, 0, None)

        def two(self):
            self.wait("zz0")
            self.push("yzz0", 0, 2, 0, dev(dyl=1))
            self.wait("zz1")
            self.push("yzz1", 0, 2, 1, dev(dyl=1))
            self.share(0, 2, None)

        def three(self):
            self.wait("yz-0")
            self.wait("yz-1")
            self.share(1, 3, None)
            self.wait("yz+0")
            self.wait("yz+1")
            self.share(1, 1, None)

        def four(self):
            self.wait("yzz0")
            self.wait("yzz1")
            self.share(1, 2, None)

    def full_gather(t):
        def slot(dy, dz, part):
            ref = full.at[t, lax.rem(yl + dy, 2), lax.rem(z + dz, 4) * 2 + c]
            return ref if part is None else ref.at[pl.ds(part * half, half)]

        def share(dy, dz, src):
            ref = slot(dy, dz, None)
            sib[t][(dy, dz)] = send(ref if src is None else src, ref, dev(dc=1))
            if t == 0:
                xsend(dy, dz, ref if src is None else src)

        return Gather(slot, share)

    e2_rows = t_rows // 8
    far = ((1, 1), (0, 3))

    def e2_gather(t):
        first, count = far[t]

        def slot(dy, dz, part):
            n = e2_rows // 2
            rows = pl.ds(pl.multiple_of(chip(dy, dz) * e2_rows + part * n, n), n)
            return other.at[t, pl.ds(first, count), :, c, rows]

        return Gather(slot, lambda dy, dz, src: None)

    ga, gb = full_gather(0), full_gather(1)
    ge = [e2_gather(0), e2_gather(1)]
    e2 = [[], []]
    eshare = [None, None]

    def e2_send(t):
        rows = pl.ds(pl.multiple_of(chip(0, 0) * e2_rows, e2_rows), e2_rows)
        first, count = far[t]
        for r in range(first, first + count):
            e2[t].append(
                send(
                    full.at[t, :, lax.rem(x + r + 1, 4) * 2 + c, rows],
                    other.at[t, r, :, c, rows],
                    dev(dx=r + 1),
                )
            )

    def e2_start(t):
        for copy in e2[t]:
            copy.wait_recv()
        ge[t].start()

    def e2_share(t):
        first, count = far[t]
        slot = other.at[t, pl.ds(first, count), :, c]
        eshare[t] = send(slot, slot, dev(dc=1))

    def forward(dy, dz, first=False):
        sib[0][(dy, dz)].wait_recv()
        m = chip(dy, dz)
        my, mz = lax.rem(yl + dy, 2), lax.rem(z + dz, 4) * 2

        @pl.loop(0, 4)
        def _(i):
            k, rows = i // 2, pl.ds(pl.multiple_of((i % 2) * half, half), half)
            part = nn(full[0, my, mz, rows], wi[k, pl.ds(pl.multiple_of(m * 512, 512), 256)]) + nn(
                full[0, my, mz + 1, rows], wi[k, pl.ds(pl.multiple_of(m * 512 + 256, 256), 256)]
            )
            if first:
                pre[k, rows] = part
            else:
                pre[k, rows] += part

    def backward(dy, dz, first=False):
        sib[1][(dy, dz)].wait_recv()
        m = chip(dy, dz)
        my, mz = lax.rem(yl + dy, 2), lax.rem(z + dz, 4) * 2

        @pl.loop(0, 2)
        def _(i):
            rows = pl.ds(pl.multiple_of(i * half, half), half)
            part = nt(full[1, my, mz, rows], wo[:, pl.ds(pl.multiple_of(m * 512, 512), 256)]) + nt(
                full[1, my, mz + 1, rows], wo[:, pl.ds(pl.multiple_of(m * 512 + 256, 256), 256)]
            )
            if first:
                pre[2, rows] = part
            else:
                pre[2, rows] += part

    step = 32

    def make_hidden():
        @pl.loop(0, t_rows // step)
        def _(i):
            rows = pl.ds(pl.multiple_of(i * step, step), step)
            v = pre[0, rows]
            up = pre[1, rows]
            t = jnp.tanh(ROOT * (v + 0.044715 * v * v * v))
            activated = 0.5 * v * (1.0 + t)
            slopes = 0.5 * (1.0 + t) + 0.5 * v * (1.0 - t * t) * ROOT * (
                1.0 + 3.0 * 0.044715 * v * v
            )
            act[HID, 0, rows] = (activated * up).astype(BF)
            pre[0, rows] = activated
            pre[1, rows] = up * slopes

    def make_d():
        @pl.loop(0, t_rows // step)
        def _(i):
            rows = pl.ds(pl.multiple_of(i * step, step), step)
            d = pre[2, rows]
            act[DUP, 0, rows] = (d * pre[0, rows]).astype(BF)
            act[DGATE, 0, rows] = (d * pre[1, rows]).astype(BF)

    xg = [{} for _ in PIECES]
    lo, hi = pl.ds(0, half), pl.ds(half, half)

    def xg_send(p, name, source, there, rows, device):
        q, first_col, cols = PIECES[p]
        cut = pl.ds(first_col, cols)
        xg[p][name] = send(act.at[q, source, rows, cut], act.at[q, there, rows, cut], device)

    def xg_start(p):
        xg_send(p, "a-", 0, 1, lo, dev(dx=1))
        xg_send(p, "b+", 0, 3, hi, dev(dx=3))
        xg_send(p, "b-", 0, 1, hi, dev(dx=1))
        xg_send(p, "a+", 0, 3, lo, dev(dx=3))

    def xg_relay(p):
        xg[p]["a-"].wait_recv()
        xg_send(p, "aa", 1, 2, lo, dev(dx=1))
        xg[p]["b+"].wait_recv()
        xg_send(p, "bb", 3, 2, hi, dev(dx=3))

    def xg_rest(p):
        xg[p]["b-"].wait_recv()
        xg[p]["a+"].wait_recv()

    def xg_last(p):
        xg[p]["aa"].wait_recv()
        xg[p]["bb"].wait_recv()

    osib = []

    def other_share():
        for r in (0, 2):
            for h in range(2):
                slot = other.at[0, r, h, c]
                pltpu.make_async_remote_copy(
                    src_ref=slot, dst_ref=slot, send_sem=xssem.at[0],
                    recv_sem=xrsem.at[r // 2, h], device_id=dev(dc=1), device_id_type=MESH,
                ).wait_recv()
            slot = other.at[0, r, :, c]
            osib.append(send(slot, slot, dev(dc=1)))

    def other_wait(t):
        eshare[t].wait_recv()
        if t == 0:
            for copy in osib:
                copy.wait_recv()

    gs = [None] * len(PIECES)

    def wgrad(p, *sources, first=False, last=False):
        q, first_col, n = PIECES[p]
        cut = pl.ds(first_col, n)
        t = 1 if q == HID else 0

        @pl.loop(0, 4)
        def _(i):
            part_kept, b = i // 2, i % 2
            h = jnp.where(part_kept == 1, yh, 1 - yh)
            rows = pl.ds(pl.multiple_of(b * 256, 256), 256)
            part = None
            for r in sources:
                left = full[t, h, 2 * x + b] if r == 0 else other[t, r - 1, h, b]
                term = tn(left, act[q, r, :, cut])
                part = term if part is None else part + term

            @pl.when(part_kept == 1)
            def _():
                pre[q, rows, cut] = part if first else pre[q, rows, cut] + part

            @pl.when(part_kept == 0)
            def _():
                total = part if first else accs[rows, cut] + part
                if last:
                    gsend[q, rows, cut] = (total * factor).astype(BF)
                else:
                    accs[rows, cut] = total

        if last:
            gs[p] = send(gsend.at[q, :, cut], grecv.at[q, :, cut], dev(dyh=1))

    def shard_rows(shard):
        return pl.ds(pl.multiple_of(shard * 256, 256), 256)

    igc = [None] * 8

    def ig_other(n, m):
        shard = 2 * m + 1 - c
        igs[m] = (
            nt(act[DGATE, 0], wi[0, shard_rows(shard)]) + nt(act[DUP, 0], wi[1, shard_rows(shard)])
        ).astype(BF)
        igc[n] = send(igs.at[m], igr.at[m], dev(dc=1))

    igzc = {}

    def ig_own(n, m):
        igc[n].wait_recv()
        shard = 2 * m + c
        total = nt(act[DGATE, 0], wi[0, shard_rows(shard)]) + nt(act[DUP, 0], wi[1, shard_rows(shard)])
        igr[m] = (total + igr[m].astype(F32)).astype(BF)

    def ig_final_1():
        for copy in igzc.values():
            copy.wait_recv()
        for y in (1, 0):
            m = chip(y, 0)
            total = igr[m].astype(F32)
            for r in range(3):
                total = total + igz[r, y].astype(F32)
            if y == 1:
                igy[0] = total.astype(BF)
                igzc["y"] = send(igy.at[0], igy.at[1], dev(dyl=1))
            else:
                rowm[2], rowm[3] = total[:, :128], total[:, 128:]

    def ig_final_2():
        igzc["y"].wait_recv()
        for i in range(2):
            cols = pl.ds(i * 128, 128)
            ig_o[:, cols] = (rowm[2 + i] + igy[1, :, cols].astype(F32)).astype(BF)

    fin = 64

    def final(p):
        q, first_col, n = PIECES[p]
        cut = pl.ds(first_col, n)
        gs[p].wait_recv()
        col = row_out[...].reshape(1, h_cols) if q == HID else col_in[pl.ds(2 - q, 1), cut]

        def body(i, colmax):
            rows = pl.ds(pl.multiple_of(i * fin, fin), fin)
            g = pre[q, rows, cut] * factor + grecv[q, rows, cut].astype(F32)
            nu = jnp.minimum(rowv[q, rows][:, :1], col) + g * g
            upd = g * lax.rsqrt(nu)
            if q == HID:
                pre[q, rows] = upd
            else:
                upd_in_o[2 - q, rows, cut] = upd.astype(BF)
            rowm[p, rows] = jnp.broadcast_to(jnp.max(nu, axis=1, keepdims=True), (fin, 128))
            return jnp.maximum(colmax, jnp.max(nu, axis=0, keepdims=True))

        colmax = lax.fori_loop(0, 512 // fin, body, jnp.zeros((1, n), F32))
        cbuf[0, pl.ds(q, 1), cut] = colmax
        rowmax = rowm[p].T[:1]
        if first_col != 0:
            rowmax = jnp.maximum(rowmax, rbuf[0, pl.ds(q, 1), pl.ds(0, 512)])
        rbuf[0, pl.ds(q, 1), pl.ds(0, 512)] = rowmax
        if q == HID:
            @pl.loop(0, h_cols // 128)
            def _(j):
                cols = pl.ds(pl.multiple_of(j * 128, 128), 128)
                upd_out_o[cols] = pre[q, :, cols].T.astype(BF)

    pl.semaphore_wait(barrier, len(peers))
    ga.start(tok_in)
    load_w = [load(w_in.at[0], wi.at[0]), load(w_in.at[1], wi.at[1])]
    cbuf[0] = jnp.zeros_like(cbuf[0])
    rbuf[0] = jnp.zeros_like(rbuf[0])
    for q in range(3):
        row = col_out[...].reshape(1, 512) if q == HID else row_in[pl.ds(2 - q, 1)]
        rowv[q] = jnp.broadcast_to(row, (128, 512)).T
    own_tok.wait()
    own_cot.wait()
    ga.one()
    gb.start(cot_in)
    load_wo = load(w_out, wo)
    ga.two()
    for copy in load_w:
        copy.wait()
    forward(0, 0, first=True)
    forward(0, 3)
    forward(0, 1)
    ga.three()
    forward(1, 0)
    ga.four()
    e2_send(0)
    forward(0, 2)
    forward(1, 3)
    forward(1, 1)
    forward(1, 2)
    make_hidden()
    xg_start(0)
    gb.one()
    load_wo.wait()
    backward(0, 0, first=True)
    gb.two()
    e2_start(0)
    backward(0, 3)
    backward(0, 1)
    gb.three()
    ge[0].one()
    backward(1, 0)
    gb.four()
    e2_send(1)
    xg_relay(0)
    ge[0].two()
    backward(0, 2)
    backward(1, 3)
    e2_start(1)
    backward(1, 1)
    backward(1, 2)
    make_d()
    xg_start(1)
    order = [(dy, dz) for dz in (2, 1, 3, 0) for dy in (1, 0)]
    for n, (dy, dz) in enumerate(order):
        ig_other(n, chip(dy, dz))
        if n == 3:
            ge[1].one()

    def ig_send(numbers):
        for n in numbers:
            dy, dz = order[n]
            ig_own(n, chip(dy, dz))
            if dz != 0:
                igzc[(dy, dz)] = send(igr.at[chip(dy, dz)], igz.at[dz - 1, dy], dev(dz=dz))

    ge[1].two()
    wgrad(0, 0, first=True)
    ge[0].three()
    ge[0].four()
    e2_share(0)
    other_share()
    ig_send((0, 1))
    ge[1].three()
    ge[1].four()
    e2_share(1)
    xg_rest(0)
    xg_last(0)
    xg_relay(1)
    xg_start(2)
    other_wait(1)
    wgrad(0, 1, 2, 3, last=True)
    ig_send((2, 3, 4, 5, 6, 7))
    other_wait(0)
    wgrad(1, 0, first=True)
    xg_rest(1)
    wgrad(1, 1, 3)
    xg_last(1)
    wgrad(1, 2, last=True)
    wgrad(2, 0, first=True)
    xg_relay(2)
    xg_start(3)
    final(0)
    load(upd_out_o, upd_out_h)
    xg_rest(2)
    wgrad(2, 1, 3)
    xg_last(2)
    wgrad(2, 2, last=True)
    wgrad(3, 0, first=True)
    xg_relay(3)
    ig_final_1()
    xg_rest(3)
    wgrad(3, 1, 3)
    xg_last(3)
    wgrad(3, 2, last=True)
    ig_final_2()
    load(ig_o, ig_h)
    final(1)
    load(upd_in_o.at[1], upd_in_h.at[1])
    final(2)
    final(3)
    load(upd_in_o.at[0], upd_in_h.at[0])

    first = [
        send(rbuf.at[0], rbuf.at[1], dev(dc=1)),
        send(rbuf.at[0], rbuf.at[2], dev(dyl=1)),
        send(rbuf.at[0], rbuf.at[3], dev(dyl=1, dc=1)),
        send(cbuf.at[0], cbuf.at[1], dev(dyh=1)),
    ]
    for copy in first:
        copy.wait_recv()
    rbuf[4] = jnp.maximum(jnp.maximum(rbuf[0], rbuf[1]), jnp.maximum(rbuf[2], rbuf[3]))
    cbuf[2] = jnp.maximum(cbuf[0], cbuf[1])
    second = []
    for r in range(1, 4):
        second.append(send(rbuf.at[4], rbuf.at[4 + r], dev(dz=r)))
        second.append(send(cbuf.at[2], cbuf.at[2 + r], dev(dx=r)))
    for copy in second:
        copy.wait_recv()
    rmax_o[...] = jnp.maximum(jnp.maximum(rbuf[4], rbuf[5]), jnp.maximum(rbuf[6], rbuf[7]))
    cmax_o[...] = jnp.maximum(jnp.maximum(cbuf[2], cbuf[3]), jnp.maximum(cbuf[4], cbuf[5]))

    for copy in loads[5:]:
        copy.wait()
    for copy in sent[-SENDING:]:
        copy.wait_send()
    for taken, copy in xsent:
        @pl.when(taken)
        def _(copy=copy):
            copy.wait_send()


def finish(
    ig, upd_in, upd_out, rmax, cmax,
    ig_o, upd_in_o, upd_out_o, row_in_o, col_in_o, row_out_o, col_out_o,
    ig_v, upd_in_v, upd_out_v, sem,
):
    steps = ((ig, ig_v, ig_o), (upd_in, upd_in_v, upd_in_o), (upd_out, upd_out_v, upd_out_o))
    ins = [pltpu.make_async_copy(s, v, sem.at[0, i]) for i, (s, v, o) in enumerate(steps)]
    copies = [pltpu.make_async_copy(v, o, sem.at[1, i]) for i, (s, v, o) in enumerate(steps)]
    for copy in ins:
        copy.start()
    n = row_in_o.shape[1]
    col_out_o[...] = rmax[HID, pl.ds(0, n)]
    row_out_o[...] = cmax[HID]
    for q in (DUP, DGATE):
        row_in_o[pl.ds(2 - q, 1)] = rmax[q : q + 1, :n]
        col_in_o[pl.ds(2 - q, 1)] = cmax[q : q + 1]
    for before, copy in zip(ins, copies):
        before.wait()
        copy.start()
    for copy in copies:
        copy.wait()


def local(tokens, cotangent, w_in, w_out, row_in, col_in, row_out, col_out):
    t_rows, d_cols = tokens.shape
    h_cols = w_out.shape[0]
    factor = 1.0 / math.sqrt(t_rows * lax.axis_size("dp"))
    vmem = pl.BlockSpec(memory_space=pltpu.VMEM)
    hbm = pl.BlockSpec(memory_space=pl.ANY)
    shapes = (
        jax.ShapeDtypeStruct((t_rows, 256), BF),
        jax.ShapeDtypeStruct((2, 512, h_cols), BF),
        jax.ShapeDtypeStruct((h_cols, 512), BF),
        jax.ShapeDtypeStruct((8, h_cols), F32),
        jax.ShapeDtypeStruct((8, h_cols), F32),
    )
    out = pl.pallas_call(
        functools.partial(kernel, factor),
        out_shape=shapes,
        in_specs=[hbm] * 4 + [vmem] * 4,
        out_specs=[hbm] * 3 + [vmem] * 2,
        scratch_shapes=[
            pltpu.VMEM((2, 2, 8, t_rows, 256), BF),
            pltpu.VMEM(w_in.shape, BF),
            pltpu.VMEM(w_out.shape, BF),
            pltpu.VMEM((3, t_rows, h_cols), F32),
            pltpu.VMEM((3, 4, t_rows, h_cols), BF),
            pltpu.VMEM((2, 3, 2, 2, t_rows, 256), BF),
            pltpu.VMEM((512, h_cols), F32),
            pltpu.VMEM((3, 512, h_cols), BF),
            pltpu.VMEM((3, 512, h_cols), BF),
            pltpu.VMEM((8, t_rows, 256), BF),
            pltpu.VMEM((8, t_rows, 256), BF),
            pltpu.VMEM((3, 2, t_rows, 256), BF),
            pltpu.VMEM((2, t_rows, 256), BF),
            pltpu.VMEM((3, 512, 128), F32),
            pltpu.VMEM((4, 512, 128), F32),
            pltpu.VMEM((8, 8, h_cols), F32),
            pltpu.VMEM((6, 8, h_cols), F32),
        ]
        + [pltpu.VMEM(s.shape, BF) for s in shapes[:3]]
        + [
            pltpu.SemaphoreType.DMA((9,)),
            pltpu.SemaphoreType.DMA((SENDING,)),
            pltpu.SemaphoreType.DMA((MESSAGES,)),
            pltpu.SemaphoreType.DMA((8,)),
            pltpu.SemaphoreType.DMA((2, 2)),
        ],
        compiler_params=pltpu.CompilerParams(
            collective_id=0, has_side_effects=True, vmem_limit_bytes=62 * 2**20
        ),
        cost_estimate=pl.CostEstimate(
            flops=21_500_000_000, bytes_accessed=22_000_000, transcendentals=330_000
        ),
    )(tokens, cotangent, w_in, w_out, row_in, col_in, row_out, col_out)
    return pl.pallas_call(
        finish,
        out_shape=shapes[:3]
        + (
            jax.ShapeDtypeStruct(row_in.shape, F32),
            jax.ShapeDtypeStruct(col_in.shape, F32),
            jax.ShapeDtypeStruct(row_out.shape, F32),
            jax.ShapeDtypeStruct(col_out.shape, F32),
        ),
        in_specs=[hbm] * 3 + [vmem] * 2,
        out_specs=[hbm] * 3 + [vmem] * 4,
        scratch_shapes=[pltpu.VMEM(s.shape, BF) for s in shapes[:3]]
        + [pltpu.SemaphoreType.DMA((2, 3))],
    )(*out)


def solution(mesh):
    return jax.shard_map(
        local,
        mesh=mesh,
        in_specs=(
            P("dp", "mp"),
            P("dp", "mp"),
            P(None, None, "mp"),
            P("mp", None),
            P(None, "dp"),
            P(None, "mp"),
            P("mp"),
            P("dp"),
        ),
        out_specs=(
            P("dp", "mp"),
            P(None, "dp", "mp"),
            P("mp", "dp"),
            P(None, "dp"),
            P(None, "mp"),
            P("mp"),
            P("dp"),
        ),
        check_vma=False,
    )
```

```python
import functools
import math

import jax
import jax.numpy as jnp
from jax import lax
from jax.experimental import pallas as pl
from jax.experimental.pallas import tpu as pltpu
from jax.sharding import PartitionSpec as P

BF = jnp.bfloat16
F32 = jnp.float32
MESH = pl.DeviceIdType.MESH
ROOT = math.sqrt(2.0 / math.pi)

HID, DUP, DGATE = 0, 1, 2
MESSAGES = 133
SENDING = 48
PIECES = ((HID, 0, 640), (DUP, 0, 640), (DGATE, 0, 384), (DGATE, 384, 256))


def nn(a, b):
    return jnp.dot(a, b, preferred_element_type=F32)


def nt(a, b):
    return lax.dot_general(a, b, (((1,), (1,)), ((), ())), preferred_element_type=F32)


def tn(a, b):
    return lax.dot_general(a, b, (((0,), (0,)), ((), ())), preferred_element_type=F32)


def kernel(
    factor,
    tok_in,
    cot_in,
    w_in,
    w_out,
    row_in_h,
    col_in_h,
    row_out_h,
    col_out_h,
    ig_h,
    upd_in_h,
    upd_out_h,
    rmax_o,
    cmax_o,
    full,
    wi,
    wo,
    pre,
    act,
    other,
    accs,
    gsend,
    grecv,
    igs,
    igr,
    igz,
    igy,
    rowv,
    rowm,
    rbuf,
    cbuf,
    ig_o,
    upd_in_o,
    upd_out_o,
    row_in,
    col_in,
    row_out,
    col_out,
    lsem,
    ssem,
    rsem,
    xssem,
    xrsem,
):
    dp, mp = lax.axis_index("dp"), lax.axis_index("mp")
    yh, x = dp // 4, dp % 4
    yl, z, c = mp // 8, (mp // 2) % 4, mp % 2
    t_rows, h_cols = pre.shape[1], pre.shape[2]
    half = t_rows // 2

    def dev(dx=0, dyh=0, dyl=0, dz=0, dc=0):
        return (
            lax.rem(yh + dyh, 2) * 4 + lax.rem(x + dx, 4),
            lax.rem(yl + dyl, 2) * 8 + lax.rem(z + dz, 4) * 2 + lax.rem(c + dc, 2),
        )

    def chip(dy, dz):
        return lax.rem(yl + dy, 2) * 4 + lax.rem(z + dz, 4)

    peers = [
        dev(dz=1), dev(dz=3), dev(dz=2), dev(dyl=1), dev(dc=1), dev(dyl=1, dc=1),
        dev(dx=1), dev(dx=3), dev(dx=2), dev(dyh=1),
    ]
    barrier = pltpu.get_barrier_semaphore()
    for peer in peers:
        pl.semaphore_signal(barrier, inc=1, device_id=peer, device_id_type=MESH)

    loads = []

    def load(src, dst):
        copy = pltpu.make_async_copy(src, dst, lsem.at[len(loads)])
        copy.start()
        loads.append(copy)
        return copy

    own_tok = load(tok_in, full.at[0, yl, z * 2 + c])
    own_cot = load(cot_in, full.at[1, yl, z * 2 + c])
    load_small = [
        load(row_in_h, row_in), load(col_in_h, col_in),
        load(row_out_h, row_out), load(col_out_h, col_out),
    ]

    sent = []

    def send(src, dst, device):
        i = len(sent)
        if i >= SENDING:
            sent[i - SENDING].wait_send()
        copy = pltpu.make_async_remote_copy(
            src_ref=src, dst_ref=dst, send_sem=ssem.at[i % SENDING], recv_sem=rsem.at[i],
            device_id=device, device_id_type=MESH,
        )
        copy.start()
        sent.append(copy)
        return copy

    xsent = []

    def xsend(dy, dz, src):
        origin_z = lax.rem(z + dz, 4)
        origin_y = lax.rem(yl + dy, 2)
        dx = lax.rem(origin_z + 4 - x, 4)
        there = dx // 2 * 2
        i = len(xsent)
        copy = pltpu.make_async_remote_copy(
            src_ref=src,
            dst_ref=other.at[0, there, origin_y, c],
            send_sem=xssem.at[i], recv_sem=xrsem.at[there // 2, origin_y],
            device_id=(yh * 4 + origin_z, mp), device_id_type=MESH,
        )
        xsent.append((dx % 2 == 1, copy))

        @pl.when(dx % 2 == 1)
        def _():
            copy.start()

    sib = [{}, {}]

    class Gather:
        def __init__(self, slot, share):
            self.slot, self.share, self.got = slot, share, {}

        def push(self, name, dy, dz, part, device, src=None):
            slot = self.slot(dy, dz, part)
            self.got[name] = send(slot if src is None else self.part_of(src, part), slot, device)

        def part_of(self, src, part):
            n = src.shape[0] // 2
            return src.at[pl.ds(part * n, n)]

        def wait(self, name):
            self.got[name].wait_recv()

        def start(self, src=None):
            self.push("z-0", 0, 0, 0, dev(dz=1), src)
            self.push("z+1", 0, 0, 1, dev(dz=3), src)
            self.push("y0", 0, 0, 0, dev(dyl=1), src)
            self.push("z-1", 0, 0, 1, dev(dz=1), src)
            self.push("z+0", 0, 0, 0, dev(dz=3), src)
            self.push("y1", 0, 0, 1, dev(dyl=1), src)
            self.share(0, 0, src)

        def one(self):
            self.wait("z-0")
            self.push("zz0", 0, 3, 0, dev(dz=1))
            self.wait("z+1")
            self.push("zz1", 0, 1, 1, dev(dz=3))
            self.wait("y0")
            self.push("yz-0", 1, 0, 0, dev(dz=1))
            self.push("yz+0", 1, 0, 0, dev(dz=3))
            self.wait("z-1")
            self.share(0, 3, None)
            self.wait("z+0")
            self.share(0, 1, None)
            self.wait("y1")
            self.push("yz-1", 1, 0, 1, dev(dz=1))
            self.push("yz+1", 1, 0, 1, dev(dz=3))
            self.share(1, 0, None)

        def two(self):
            self.wait("zz0")
            self.push("yzz0", 0, 2, 0, dev(dyl=1))
            self.wait("zz1")
            self.push("yzz1", 0, 2, 1, dev(dyl=1))
            self.share(0, 2, None)

        def three(self):
            self.wait("yz-0")
            self.wait("yz-1")
            self.share(1, 3, None)
            self.wait("yz+0")
            self.wait("yz+1")
            self.share(1, 1, None)

        def four(self):
            self.wait("yzz0")
            self.wait("yzz1")
            self.share(1, 2, None)

    def full_gather(t):
        def slot(dy, dz, part):
            ref = full.at[t, lax.rem(yl + dy, 2), lax.rem(z + dz, 4) * 2 + c]
            return ref if part is None else ref.at[pl.ds(part * half, half)]

        def share(dy, dz, src):
            ref = slot(dy, dz, None)
            sib[t][(dy, dz)] = send(ref if src is None else src, ref, dev(dc=1))
            if t == 0:
                xsend(dy, dz, ref if src is None else src)

        return Gather(slot, share)

    e2_rows = t_rows // 8
    far = ((1, 1), (0, 3))

    def e2_gather(t):
        first, count = far[t]

        def slot(dy, dz, part):
            n = e2_rows // 2
            rows = pl.ds(pl.multiple_of(chip(dy, dz) * e2_rows + part * n, n), n)
            return other.at[t, pl.ds(first, count), :, c, rows]

        return Gather(slot, lambda dy, dz, src: None)

    ga, gb = full_gather(0), full_gather(1)
    ge = [e2_gather(0), e2_gather(1)]
    e2 = [[], []]
    eshare = [None, None]

    def e2_send(t):
        rows = pl.ds(pl.multiple_of(chip(0, 0) * e2_rows, e2_rows), e2_rows)
        first, count = far[t]
        for r in range(first, first + count):
            e2[t].append(
                send(
                    full.at[t, :, lax.rem(x + r + 1, 4) * 2 + c, rows],
                    other.at[t, r, :, c, rows],
                    dev(dx=r + 1),
                )
            )

    def e2_start(t):
        for copy in e2[t]:
            copy.wait_recv()
        ge[t].start()

    def e2_share(t):
        first, count = far[t]
        slot = other.at[t, pl.ds(first, count), :, c]
        eshare[t] = send(slot, slot, dev(dc=1))

    def forward(dy, dz, first=False):
        sib[0][(dy, dz)].wait_recv()
        m = chip(dy, dz)
        my, mz = lax.rem(yl + dy, 2), lax.rem(z + dz, 4) * 2

        @pl.loop(0, 4)
        def _(i):
            k, rows = i // 2, pl.ds(pl.multiple_of((i % 2) * half, half), half)
            part = nn(full[0, my, mz, rows], wi[k, pl.ds(pl.multiple_of(m * 512, 512), 256)]) + nn(
                full[0, my, mz + 1, rows], wi[k, pl.ds(pl.multiple_of(m * 512 + 256, 256), 256)]
            )
            if first:
                pre[k, rows] = part
            else:
                pre[k, rows] += part

    def backward(dy, dz, first=False):
        sib[1][(dy, dz)].wait_recv()
        m = chip(dy, dz)
        my, mz = lax.rem(yl + dy, 2), lax.rem(z + dz, 4) * 2

        @pl.loop(0, 2)
        def _(i):
            rows = pl.ds(pl.multiple_of(i * half, half), half)
            part = nt(full[1, my, mz, rows], wo[:, pl.ds(pl.multiple_of(m * 512, 512), 256)]) + nt(
                full[1, my, mz + 1, rows], wo[:, pl.ds(pl.multiple_of(m * 512 + 256, 256), 256)]
            )
            if first:
                pre[2, rows] = part
            else:
                pre[2, rows] += part

    step = 32

    def make_hidden():
        @pl.loop(0, t_rows // step)
        def _(i):
            rows = pl.ds(pl.multiple_of(i * step, step), step)
            v = pre[0, rows]
            up = pre[1, rows]
            t = jnp.tanh(ROOT * (v + 0.044715 * v * v * v))
            activated = 0.5 * v * (1.0 + t)
            slopes = 0.5 * (1.0 + t) + 0.5 * v * (1.0 - t * t) * ROOT * (
                1.0 + 3.0 * 0.044715 * v * v
            )
            act[HID, 0, rows] = (activated * up).astype(BF)
            pre[0, rows] = activated
            pre[1, rows] = up * slopes

    def make_d():
        @pl.loop(0, t_rows // step)
        def _(i):
            rows = pl.ds(pl.multiple_of(i * step, step), step)
            d = pre[2, rows]
            act[DUP, 0, rows] = (d * pre[0, rows]).astype(BF)
            act[DGATE, 0, rows] = (d * pre[1, rows]).astype(BF)

    xg = [{} for _ in PIECES]
    lo, hi = pl.ds(0, half), pl.ds(half, half)

    def xg_send(p, name, source, there, rows, device):
        q, first_col, cols = PIECES[p]
        cut = pl.ds(first_col, cols)
        xg[p][name] = send(act.at[q, source, rows, cut], act.at[q, there, rows, cut], device)

    def xg_start(p):
        xg_send(p, "a-", 0, 1, lo, dev(dx=1))
        xg_send(p, "b+", 0, 3, hi, dev(dx=3))
        xg_send(p, "b-", 0, 1, hi, dev(dx=1))
        xg_send(p, "a+", 0, 3, lo, dev(dx=3))

    def xg_relay(p):
        xg[p]["a-"].wait_recv()
        xg_send(p, "aa", 1, 2, lo, dev(dx=1))
        xg[p]["b+"].wait_recv()
        xg_send(p, "bb", 3, 2, hi, dev(dx=3))

    def xg_rest(p):
        xg[p]["b-"].wait_recv()
        xg[p]["a+"].wait_recv()

    def xg_last(p):
        xg[p]["aa"].wait_recv()
        xg[p]["bb"].wait_recv()

    osib = []

    def other_share():
        for r in (0, 2):
            for h in range(2):
                slot = other.at[0, r, h, c]
                pltpu.make_async_remote_copy(
                    src_ref=slot, dst_ref=slot, send_sem=xssem.at[0],
                    recv_sem=xrsem.at[r // 2, h], device_id=dev(dc=1), device_id_type=MESH,
                ).wait_recv()
            slot = other.at[0, r, :, c]
            osib.append(send(slot, slot, dev(dc=1)))

    def other_wait(t):
        eshare[t].wait_recv()
        if t == 0:
            for copy in osib:
                copy.wait_recv()

    gs = [None] * len(PIECES)

    def wgrad(p, *sources, first=False, last=False):
        q, first_col, n = PIECES[p]
        cut = pl.ds(first_col, n)
        t = 1 if q == HID else 0

        @pl.loop(0, 4)
        def _(i):
            part_kept, b = i // 2, i % 2
            h = jnp.where(part_kept == 1, yh, 1 - yh)
            rows = pl.ds(pl.multiple_of(b * 256, 256), 256)
            part = None
            for r in sources:
                left = full[t, h, 2 * x + b] if r == 0 else other[t, r - 1, h, b]
                term = tn(left, act[q, r, :, cut])
                part = term if part is None else part + term

            @pl.when(part_kept == 1)
            def _():
                pre[q, rows, cut] = part if first else pre[q, rows, cut] + part

            @pl.when(part_kept == 0)
            def _():
                total = part if first else accs[rows, cut] + part
                if last:
                    gsend[q, rows, cut] = (total * factor).astype(BF)
                else:
                    accs[rows, cut] = total

        if last:
            gs[p] = send(gsend.at[q, :, cut], grecv.at[q, :, cut], dev(dyh=1))

    def shard_rows(shard):
        return pl.ds(pl.multiple_of(shard * 256, 256), 256)

    igc = [None] * 8

    def ig_other(n, m):
        shard = 2 * m + 1 - c
        igs[m] = (
            nt(act[DGATE, 0], wi[0, shard_rows(shard)]) + nt(act[DUP, 0], wi[1, shard_rows(shard)])
        ).astype(BF)
        igc[n] = send(igs.at[m], igr.at[m], dev(dc=1))

    igzc = {}

    def ig_own(n, m):
        igc[n].wait_recv()
        shard = 2 * m + c
        total = nt(act[DGATE, 0], wi[0, shard_rows(shard)]) + nt(act[DUP, 0], wi[1, shard_rows(shard)])
        igr[m] = (total + igr[m].astype(F32)).astype(BF)

    def ig_final_1():
        for copy in igzc.values():
            copy.wait_recv()
        for y in (1, 0):
            m = chip(y, 0)
            total = igr[m].astype(F32)
            for r in range(3):
                total = total + igz[r, y].astype(F32)
            if y == 1:
                igy[0] = total.astype(BF)
                igzc["y"] = send(igy.at[0], igy.at[1], dev(dyl=1))
            else:
                rowm[2], rowm[3] = total[:, :128], total[:, 128:]

    def ig_final_2():
        igzc["y"].wait_recv()
        for i in range(2):
            cols = pl.ds(i * 128, 128)
            ig_o[:, cols] = (rowm[2 + i] + igy[1, :, cols].astype(F32)).astype(BF)

    fin = 64

    def final(p):
        q, first_col, n = PIECES[p]
        cut = pl.ds(first_col, n)
        gs[p].wait_recv()
        col = row_out[...].reshape(1, h_cols) if q == HID else col_in[pl.ds(2 - q, 1), cut]

        def body(i, colmax):
            rows = pl.ds(pl.multiple_of(i * fin, fin), fin)
            g = pre[q, rows, cut] * factor + grecv[q, rows, cut].astype(F32)
            nu = jnp.minimum(rowv[q, rows][:, :1], col) + g * g
            upd = g * lax.rsqrt(nu)
            if q == HID:
                pre[q, rows] = upd
            else:
                upd_in_o[2 - q, rows, cut] = upd.astype(BF)
            rowm[p, rows] = jnp.broadcast_to(jnp.max(nu, axis=1, keepdims=True), (fin, 128))
            return jnp.maximum(colmax, jnp.max(nu, axis=0, keepdims=True))

        colmax = lax.fori_loop(0, 512 // fin, body, jnp.zeros((1, n), F32))
        cbuf[0, pl.ds(q, 1), cut] = colmax
        rowmax = rowm[p].T[:1]
        if first_col != 0:
            rowmax = jnp.maximum(rowmax, rbuf[0, pl.ds(q, 1), pl.ds(0, 512)])
        rbuf[0, pl.ds(q, 1), pl.ds(0, 512)] = rowmax
        if q == HID:
            @pl.loop(0, h_cols // 128)
            def _(j):
                cols = pl.ds(pl.multiple_of(j * 128, 128), 128)
                upd_out_o[cols] = pre[q, :, cols].T.astype(BF)

    pl.semaphore_wait(barrier, len(peers))
    ga.start(tok_in)
    load_w = [load(w_in.at[0], wi.at[0]), load(w_in.at[1], wi.at[1])]
    cbuf[0] = jnp.zeros_like(cbuf[0])
    rbuf[0] = jnp.zeros_like(rbuf[0])
    for copy in load_small:
        copy.wait()
    for q in range(3):
        row = col_out[...].reshape(1, 512) if q == HID else row_in[pl.ds(2 - q, 1)]
        rowv[q] = jnp.broadcast_to(row, (128, 512)).T
    own_tok.wait()
    own_cot.wait()
    ga.one()
    gb.start(cot_in)
    load_wo = load(w_out, wo)
    ga.two()
    for copy in load_w:
        copy.wait()
    forward(0, 0, first=True)
    forward(0, 3)
    forward(0, 1)
    ga.three()
    forward(1, 0)
    ga.four()
    e2_send(0)
    forward(0, 2)
    forward(1, 3)
    forward(1, 1)
    forward(1, 2)
    make_hidden()
    xg_start(0)
    gb.one()
    load_wo.wait()
    backward(0, 0, first=True)
    gb.two()
    e2_start(0)
    backward(0, 3)
    backward(0, 1)
    gb.three()
    ge[0].one()
    backward(1, 0)
    gb.four()
    e2_send(1)
    xg_relay(0)
    ge[0].two()
    backward(0, 2)
    backward(1, 3)
    e2_start(1)
    backward(1, 1)
    backward(1, 2)
    make_d()
    xg_start(1)
    order = [(dy, dz) for dz in (2, 1, 3, 0) for dy in (1, 0)]
    for n, (dy, dz) in enumerate(order):
        ig_other(n, chip(dy, dz))
        if n == 3:
            ge[1].one()
            wgrad(0, 0, first=True)
            ge[1].two()

    def ig_send(numbers):
        for n in numbers:
            dy, dz = order[n]
            ig_own(n, chip(dy, dz))
            if dz != 0:
                igzc[(dy, dz)] = send(igr.at[chip(dy, dz)], igz.at[dz - 1, dy], dev(dz=dz))

    ge[0].three()
    ge[0].four()
    e2_share(0)
    other_share()
    ge[1].three()
    ge[1].four()
    e2_share(1)
    xg_rest(0)
    xg_last(0)
    xg_relay(1)
    xg_start(2)
    other_wait(1)
    wgrad(0, 1, 2, 3, last=True)
    ig_send(range(8))
    other_wait(0)
    wgrad(1, 0, first=True)
    xg_rest(1)
    wgrad(1, 1, 3)
    xg_last(1)
    wgrad(1, 2, last=True)
    wgrad(2, 0, first=True)
    xg_relay(2)
    xg_start(3)
    final(0)
    load(upd_out_o, upd_out_h)
    xg_rest(2)
    wgrad(2, 1, 3)
    xg_last(2)
    wgrad(2, 2, last=True)
    wgrad(3, 0, first=True)
    xg_relay(3)
    ig_final_1()
    xg_rest(3)
    wgrad(3, 1, 3)
    xg_last(3)
    wgrad(3, 2, last=True)
    ig_final_2()
    load(ig_o, ig_h)
    final(1)
    load(upd_in_o.at[1], upd_in_h.at[1])
    final(2)
    final(3)
    load(upd_in_o.at[0], upd_in_h.at[0])

    first = [
        send(rbuf.at[0], rbuf.at[1], dev(dc=1)),
        send(rbuf.at[0], rbuf.at[2], dev(dyl=1)),
        send(rbuf.at[0], rbuf.at[3], dev(dyl=1, dc=1)),
        send(cbuf.at[0], cbuf.at[1], dev(dyh=1)),
    ]
    for copy in first:
        copy.wait_recv()
    rbuf[4] = jnp.maximum(jnp.maximum(rbuf[0], rbuf[1]), jnp.maximum(rbuf[2], rbuf[3]))
    cbuf[2] = jnp.maximum(cbuf[0], cbuf[1])
    second = []
    for r in range(1, 4):
        second.append(send(rbuf.at[4], rbuf.at[4 + r], dev(dz=r)))
        second.append(send(cbuf.at[2], cbuf.at[2 + r], dev(dx=r)))
    for copy in second:
        copy.wait_recv()
    rmax_o[...] = jnp.maximum(jnp.maximum(rbuf[4], rbuf[5]), jnp.maximum(rbuf[6], rbuf[7]))
    cmax_o[...] = jnp.maximum(jnp.maximum(cbuf[2], cbuf[3]), jnp.maximum(cbuf[4], cbuf[5]))

    for copy in loads[9:]:
        copy.wait()
    for copy in sent[-SENDING:]:
        copy.wait_send()
    for taken, copy in xsent:
        @pl.when(taken)
        def _(copy=copy):
            copy.wait_send()


def finish(
    ig, upd_in, upd_out, rmax, cmax,
    ig_o, upd_in_o, upd_out_o, row_in_o, col_in_o, row_out_o, col_out_o,
    ig_v, upd_in_v, upd_out_v, rmax_v, cmax_v, row_in_v, col_in_v, row_out_v, col_out_v, sem,
):
    ins = ((rmax, rmax_v), (cmax, cmax_v), (ig, ig_v), (upd_out, upd_out_v), (upd_in, upd_in_v))
    ins = [pltpu.make_async_copy(s, d, sem.at[i]) for i, (s, d) in enumerate(ins)]
    for copy in ins:
        copy.start()
    big = ((ig_v, ig_o), (upd_out_v, upd_out_o), (upd_in_v, upd_in_o))
    small = (
        (row_in_v, row_in_o), (col_in_v, col_in_o), (row_out_v, row_out_o), (col_out_v, col_out_o)
    )
    outs = [pltpu.make_async_copy(s, d, sem.at[5 + i]) for i, (s, d) in enumerate(small + big)]
    ins[0].wait()
    ins[1].wait()
    n = row_in_o.shape[1]
    col_out_v[...] = rmax_v[HID, pl.ds(0, n)]
    row_out_v[...] = cmax_v[HID]
    for q in (DUP, DGATE):
        row_in_v[pl.ds(2 - q, 1)] = rmax_v[q : q + 1, :n]
        col_in_v[pl.ds(2 - q, 1)] = cmax_v[q : q + 1]
    for i, copy in enumerate(outs):
        if i >= 4:
            ins[i - 2].wait()
        copy.start()
    for copy in outs:
        copy.wait()


def local(tokens, cotangent, w_in, w_out, row_in, col_in, row_out, col_out):
    t_rows, d_cols = tokens.shape
    h_cols = w_out.shape[0]
    factor = 1.0 / math.sqrt(t_rows * lax.axis_size("dp"))
    vmem = pl.BlockSpec(memory_space=pltpu.VMEM)
    hbm = pl.BlockSpec(memory_space=pl.ANY)
    shapes = (
        jax.ShapeDtypeStruct((t_rows, 256), BF),
        jax.ShapeDtypeStruct((2, 512, h_cols), BF),
        jax.ShapeDtypeStruct((h_cols, 512), BF),
        jax.ShapeDtypeStruct((8, h_cols), F32),
        jax.ShapeDtypeStruct((8, h_cols), F32),
    )
    out = pl.pallas_call(
        functools.partial(kernel, factor),
        out_shape=shapes,
        in_specs=[hbm] * 8,
        out_specs=[hbm] * 3 + [vmem] * 2,
        scratch_shapes=[
            pltpu.VMEM((2, 2, 8, t_rows, 256), BF),
            pltpu.VMEM(w_in.shape, BF),
            pltpu.VMEM(w_out.shape, BF),
            pltpu.VMEM((3, t_rows, h_cols), F32),
            pltpu.VMEM((3, 4, t_rows, h_cols), BF),
            pltpu.VMEM((2, 3, 2, 2, t_rows, 256), BF),
            pltpu.VMEM((512, h_cols), F32),
            pltpu.VMEM((3, 512, h_cols), BF),
            pltpu.VMEM((3, 512, h_cols), BF),
            pltpu.VMEM((8, t_rows, 256), BF),
            pltpu.VMEM((8, t_rows, 256), BF),
            pltpu.VMEM((3, 2, t_rows, 256), BF),
            pltpu.VMEM((2, t_rows, 256), BF),
            pltpu.VMEM((3, 512, 128), F32),
            pltpu.VMEM((4, 512, 128), F32),
            pltpu.VMEM((8, 8, h_cols), F32),
            pltpu.VMEM((6, 8, h_cols), F32),
        ]
        + [pltpu.VMEM(s.shape, BF) for s in shapes[:3]]
        + [pltpu.VMEM(a.shape, F32) for a in (row_in, col_in, row_out, col_out)]
        + [
            pltpu.SemaphoreType.DMA((13,)),
            pltpu.SemaphoreType.DMA((SENDING,)),
            pltpu.SemaphoreType.DMA((MESSAGES,)),
            pltpu.SemaphoreType.DMA((8,)),
            pltpu.SemaphoreType.DMA((2, 2)),
        ],
        compiler_params=pltpu.CompilerParams(
            collective_id=0, has_side_effects=True, vmem_limit_bytes=62 * 2**20
        ),
        cost_estimate=pl.CostEstimate(
            flops=21_500_000_000, bytes_accessed=22_000_000, transcendentals=330_000
        ),
    )(tokens, cotangent, w_in, w_out, row_in, col_in, row_out, col_out)
    return pl.pallas_call(
        finish,
        out_shape=shapes[:3]
        + (
            jax.ShapeDtypeStruct(row_in.shape, F32),
            jax.ShapeDtypeStruct(col_in.shape, F32),
            jax.ShapeDtypeStruct(row_out.shape, F32),
            jax.ShapeDtypeStruct(col_out.shape, F32),
        ),
        in_specs=[hbm] * 5,
        out_specs=[hbm] * 7,
        scratch_shapes=[pltpu.VMEM(s.shape, BF) for s in shapes[:3]]
        + [pltpu.VMEM(s.shape, F32) for s in shapes[3:]]
        + [pltpu.VMEM(a.shape, F32) for a in (row_in, col_in, row_out, col_out)]
        + [pltpu.SemaphoreType.DMA((12,))],
    )(*out)


def solution(mesh):
    return jax.shard_map(
        local,
        mesh=mesh,
        in_specs=(
            P("dp", "mp"),
            P("dp", "mp"),
            P(None, None, "mp"),
            P("mp", None),
            P(None, "dp"),
            P(None, "mp"),
            P("mp"),
            P("dp"),
        ),
        out_specs=(
            P("dp", "mp"),
            P(None, "dp", "mp"),
            P("mp", "dp"),
            P(None, "dp"),
            P(None, "mp"),
            P("mp"),
            P("dp"),
        ),
        check_vma=False,
    )
```
